128 devices in a mesh: lat: 8 (over y, z_hi), lon: 16 (over x, z_lo, core).
Axes of the slice: x: 4, y: 4, z: 4 (z_hi: 2, z_lo: 2; z = z_hi * 2 + z_lo), core: 2. Of those that a mesh axis runs over, the one named last changes fastest.
Arguments:
- tokens: bfloat16 [4, 48, 768, 512], P(None, 'lat', 'lon'), may hold values from -36 to 36
- band_ids: int32 [48], replicated, may hold values from 0 to 23, never falling along the last dimension, each value on 1 to 4 neighbouring positions
- qkv_weight: bfloat16 [512, 1536], replicated, may hold values from -16 to 16
- proj_weight: bfloat16 [512, 512], replicated, may hold values from -0.25 to 0.25
- fc1_weight: bfloat16 [512, 2048], replicated, may hold values from -0.25 to 0.25
- fc2_weight: bfloat16 [2048, 512], replicated, may hold values from -0.125 to 0.125
- merge_weight: bfloat16 [2048, 1024], replicated, may hold values from -0.125 to 0.125
Outputs:
- coarse: bfloat16 [4, 24, 1024, 384], P(None, 'lat', 'lon')
The draws below stay inside these ranges and needn't reach their ends.
Inputs may be any that keep to these rules, and one draw needn't show every extreme that they name: `band_ids`: band ids never fall along latitude, every band from 0 to 23 occurs, so the first and the last row lie in different bands.
All inputs are finite; a program needn't handle non-finite values.
Results may differ from the reference program's by a relative error of at most 0.015.
Values may be sent and summed in bfloat16 or wider, within the bound.
A program may use at most 128 MiB of HBM per device.

```python
import math
import jax
import jax.numpy as jnp
import numpy as np
from jax import lax

D = 512
HEADS = 8
FF = 2048
LEV = 4
WIN_LEV = 2
WIN_LAT = 6
WIN_LON = 12
NLAT = 48
NLON = 768
BANDS = 24


def draw_tokens(key, part):
    key = jax.random.fold_in(key, 11)
    key_rows, key_cols, key_noise = jax.random.split(key, 3)
    grid_shape = (LEV, NLAT, NLON, D)
    column_scale = jnp.exp(jax.random.uniform(key_cols, (D,), jnp.float32, math.log(0.3), math.log(3.0)))
    row_scale = jnp.exp(jax.random.uniform(key_rows, (LEV, NLAT, NLON, 1), jnp.float32, math.log(0.3), math.log(3.0)))
    raw_noise = jnp.clip(jax.random.normal(key_noise, grid_shape, jnp.float32), -4.0, 4.0)
    return (raw_noise * row_scale * column_scale).astype(jnp.bfloat16)


def draw_qkv_weight(key, part):
    key = jax.random.fold_in(key, 23)
    key_query, key_keys, key_values = jax.random.split(key, 3)
    factor = D ** (-0.5)
    query_part = jnp.clip(jax.random.normal(key_query, (D, D), jnp.float32), -4.0, 4.0) * factor
    keys_part = jnp.clip(jax.random.normal(key_keys, (D, D), jnp.float32), -4.0, 4.0) * factor
    value_part = jnp.clip(jax.random.normal(key_values, (D, D), jnp.float32), -4.0, 4.0) * factor
    return jnp.concatenate([query_part, keys_part, value_part], axis=1).astype(jnp.bfloat16)


def length_profile(number_of, total, reach, lean):
    loads = [(1 << 20) // math.isqrt(grade ** lean) + 1 for grade in range(2, number_of + 1)]
    rest, given = total - reach - (number_of - 1), [1] * (number_of - 1)
    while rest > 0:
        free = [i for i in range(number_of - 1) if given[i] < reach]
        mass, left = sum([loads[i] for i in free]), rest
        for i in free:
            extra = min(reach - given[i], max(1, left * loads[i] // mass), rest)
            given[i] = given[i] + extra
            rest = rest - extra
    return np.array([reach] + given)


def ragged(key, amount, total, limit, slope):
    if amount == 2:
        one = jax.random.randint(key, (), max(1, total - limit), min(limit, total - 1) + 1)
        return jnp.stack([one, total - one])
    lengths = jnp.asarray(length_profile(amount, total, limit, slope), jnp.int32)
    couples = (amount - 1) // 2
    giver, receiver = lengths[1:1 + 2 * couples:2], lengths[2:2 + 2 * couples:2]
    slack = jnp.minimum(giver - 1, limit - receiver)
    passed = jax.random.randint(jax.random.fold_in(key, 1), (couples,), 0, 1 << 20) % (slack + 1)
    lengths = lengths.at[1:1 + 2 * couples:2].set(giver - passed).at[2:2 + 2 * couples:2].set(receiver + passed)
    return lengths[jax.random.permutation(jax.random.fold_in(key, 2), amount)]


def scatter_about(key, extent, width, most, held_as=jnp.bfloat16):
    return jnp.clip(width * jax.random.normal(key, extent, jnp.float32), -most, most).astype(held_as)


def setup_inputs(seed: int = 0) -> dict:
    key_of = jax.random.split(jax.random.key(seed), 8)
    tokens = draw_tokens(jax.random.fold_in(key_of[7], 71), 0)
    band_ids = jnp.searchsorted(jnp.cumsum(ragged(key_of[1], BANDS, NLAT, 4, 0)), jnp.arange(NLAT), side="right").astype(jnp.int32)
    qkv_weight = draw_qkv_weight(jax.random.fold_in(key_of[7], 71), 0)
    proj_weight = scatter_about(key_of[3], (D, D), D ** -0.5, 0.25)
    fc1_weight = scatter_about(key_of[4], (D, FF), D ** -0.5, 0.25)
    fc2_weight = scatter_about(key_of[5], (FF, D), FF ** -0.5, 0.125)
    merge_weight = scatter_about(key_of[6], (4 * D, 2 * D), (4 * D) ** -0.5, 0.125)
    return dict(tokens=tokens, band_ids=band_ids, qkv_weight=qkv_weight, proj_weight=proj_weight, fc1_weight=fc1_weight, fc2_weight=fc2_weight, merge_weight=merge_weight)


def layer_norm(values):
    average = lax.optimization_barrier(jnp.mean(values, axis=-1, keepdims=True))
    centred = values - average
    spread = lax.optimization_barrier(jnp.mean(centred * centred, axis=-1, keepdims=True))
    return centred * lax.rsqrt(spread + 1e-05)

def window_attention(region, band_rows, qkv_weight, proj_weight):
    levels, lat_rows, lon_cols, model_width = region.shape
    head_count = HEADS
    head_size = model_width // head_count
    lev_win = levels // WIN_LEV
    lat_win = lat_rows // WIN_LAT
    lon_win = lon_cols // WIN_LON
    window_tokens = WIN_LEV * WIN_LAT * WIN_LON
    flattened = region.reshape(-1, model_width)
    normed = layer_norm(flattened.astype(jnp.float32)).astype(jnp.bfloat16)
    packed = jnp.dot(normed, qkv_weight, preferred_element_type=jnp.float32).astype(jnp.bfloat16)
    shaped = packed.reshape(lev_win, WIN_LEV, lat_win, WIN_LAT, lon_win, WIN_LON, 3, head_count, head_size)
    windowed = shaped.transpose(0, 2, 4, 6, 7, 1, 3, 5, 8)
    windowed = windowed.reshape(lev_win * lat_win * lon_win, 3, head_count, window_tokens, head_size)
    queries = windowed[:, 0].astype(jnp.float32)
    keyset = windowed[:, 1].astype(jnp.float32)
    valueset = windowed[:, 2].astype(jnp.float32)
    scores = jnp.einsum('whqd,whkd->whqk', queries, keyset) * head_size ** (-0.5)
    token_band = jnp.broadcast_to(band_rows.reshape(lat_win, 1, WIN_LAT, 1), (lat_win, WIN_LEV, WIN_LAT, WIN_LON))
    token_band = token_band.reshape(lat_win, window_tokens)
    allowed = token_band[:, :, None] == token_band[:, None, :]
    allowed = jnp.broadcast_to(allowed[None, :, None, None], (lev_win, lat_win, lon_win, 1, window_tokens, window_tokens))
    allowed = allowed.reshape(-1, 1, window_tokens, window_tokens)
    masked = jnp.where(allowed, scores, -jnp.inf)
    weights = jax.nn.softmax(masked, axis=-1).astype(jnp.bfloat16)
    attended = jnp.einsum('whqk,whkd->whqd', weights.astype(jnp.float32), valueset).astype(jnp.bfloat16)
    attended = attended.reshape(lev_win, lat_win, lon_win, head_count, WIN_LEV, WIN_LAT, WIN_LON, head_size)
    attended = attended.transpose(0, 4, 1, 5, 2, 6, 3, 7).reshape(-1, model_width)
    updated = flattened.astype(jnp.float32) + jnp.dot(attended, proj_weight, preferred_element_type=jnp.float32)
    return updated.astype(jnp.bfloat16).reshape(region.shape)

def feed_forward(restored, fc1_weight, fc2_weight):
    flattened = restored.reshape(-1, restored.shape[-1])
    normed = layer_norm(flattened.astype(jnp.float32)).astype(jnp.bfloat16)
    hidden = jax.nn.gelu(jnp.dot(normed, fc1_weight, preferred_element_type=jnp.float32), approximate=False).astype(jnp.bfloat16)
    result_tokens = flattened.astype(jnp.float32) + jnp.dot(hidden, fc2_weight, preferred_element_type=jnp.float32)
    return result_tokens.astype(jnp.bfloat16).reshape(restored.shape)

def patch_merge(block_out, merge_weight):
    stacked = jnp.concatenate([block_out[:, 0::2, 0::2], block_out[:, 1::2, 0::2], block_out[:, 0::2, 1::2], block_out[:, 1::2, 1::2]], axis=-1)
    normed = layer_norm(stacked.astype(jnp.float32)).astype(jnp.bfloat16)
    merged = jnp.einsum('labk,kc->lacb', normed.astype(jnp.float32), merge_weight.astype(jnp.float32))
    return merged.astype(jnp.bfloat16)

def reference(tokens, band_ids, qkv_weight, proj_weight, fc1_weight, fc2_weight, merge_weight):
    lat_rim = WIN_LAT // 2
    lon_rim = WIN_LON // 2
    shifted = jnp.roll(tokens, (-lat_rim, -lon_rim), axis=(1, 2))
    shifted_band = jnp.roll(band_ids, -lat_rim)
    band_count = NLAT // WIN_LAT
    band_blocks = shifted.reshape(LEV, band_count, WIN_LAT, NLON, D).transpose(1, 0, 2, 3, 4)
    band_table = shifted_band.reshape(band_count, WIN_LAT)

    def attend_band(operands):
        return window_attention(operands[0], operands[1], qkv_weight, proj_weight)
    updated = lax.map(attend_band, (band_blocks, band_table))
    updated = updated.transpose(1, 0, 2, 3, 4).reshape(LEV, NLAT, NLON, D)
    restored = jnp.roll(updated, (lat_rim, lon_rim), axis=(1, 2))
    row_pairs = restored.reshape(LEV, NLAT // 2, 2, NLON, D).transpose(1, 0, 2, 3, 4)

    def finish_pair(pair_block):
        return patch_merge(feed_forward(pair_block, fc1_weight, fc2_weight), merge_weight)
    merged = lax.map(finish_pair, row_pairs)
    return merged[:, :, 0].transpose(1, 0, 2, 3)
```

```python
import functools

import jax
import jax.numpy as jnp
from jax import lax
from jax.experimental import pallas as pl
from jax.experimental.pallas import tpu as pltpu
from jax.sharding import PartitionSpec as P

HEADS = 8
WIN_LEV = 2
WIN_LAT = 6
WIN_LON = 12
MESH = pl.DeviceIdType.MESH
BF16 = jnp.bfloat16
F32 = jnp.float32
PEERS = 16


def shifted_2(block, axis, distance):
    devices = range(lax.axis_size(axis))
    route = [((i - distance) % len(devices), i) for i in devices]
    return lax.ppermute(block, axis, route)


def layer_norm(values):
    average = jnp.mean(values, axis=-1, keepdims=True)
    centred = values - average
    spread = jnp.mean(centred * centred, axis=-1, keepdims=True)
    return centred * lax.rsqrt(spread + 1e-05)


def window_attention(region, band_rows, qkv_weight, proj_weight):
    levels, lat_rows, lon_cols, model_width = region.shape
    head_count = HEADS
    head_size = model_width // head_count
    lev_win = levels // WIN_LEV
    lat_win = lat_rows // WIN_LAT
    lon_win = lon_cols // WIN_LON
    window_tokens = WIN_LEV * WIN_LAT * WIN_LON
    ordered = region.reshape(lev_win, WIN_LEV, lat_win, WIN_LAT, lon_win, WIN_LON, model_width)
    ordered = ordered.transpose(0, 2, 4, 1, 3, 5, 6).reshape(-1, model_width)
    normed = layer_norm(ordered.astype(jnp.float32)).astype(jnp.bfloat16)
    packed = jnp.dot(normed, qkv_weight, preferred_element_type=jnp.float32).astype(jnp.bfloat16)
    packed = packed.reshape(lev_win * lat_win * lon_win, window_tokens, 3, head_count, head_size)
    queries = packed[:, :, 0]
    keyset = packed[:, :, 1]
    valueset = packed[:, :, 2]
    scores = jnp.einsum(
        "wqhd,wkhd->whqk", queries, keyset, preferred_element_type=jnp.float32
    ) * head_size ** (-0.5)
    token_band = jnp.broadcast_to(
        band_rows.reshape(lat_win, 1, WIN_LAT, 1), (lat_win, WIN_LEV, WIN_LAT, WIN_LON)
    )
    token_band = token_band.reshape(lat_win, window_tokens)
    allowed = token_band[:, :, None] == token_band[:, None, :]
    allowed = jnp.broadcast_to(
        allowed[None, :, None, None], (lev_win, lat_win, lon_win, 1, window_tokens, window_tokens)
    )
    allowed = allowed.reshape(-1, 1, window_tokens, window_tokens)
    masked = jnp.where(allowed, scores, -jnp.inf)
    weights = jax.nn.softmax(masked, axis=-1).astype(jnp.bfloat16)
    attended = jnp.einsum(
        "whqk,wkhd->wqhd", weights, valueset, preferred_element_type=jnp.float32
    ).astype(jnp.bfloat16)
    attended = attended.reshape(-1, model_width)
    updated = ordered.astype(jnp.float32) + jnp.dot(
        attended, proj_weight, preferred_element_type=jnp.float32
    )
    updated = updated.astype(jnp.bfloat16).reshape(
        lev_win, lat_win, lon_win, WIN_LEV, WIN_LAT, WIN_LON, model_width
    )
    return updated.transpose(0, 3, 1, 4, 2, 5, 6).reshape(region.shape)


def dot(a, b):
    return jnp.dot(a, b, preferred_element_type=F32)


def finish_group(restored, fc1, fc2, merge, acc, block):
    normed = layer_norm(restored[...].astype(F32)).astype(BF16)
    part = 512

    def step(i, carry):
        cols = pl.ds(pl.multiple_of(i * part, part), part)
        pre = dot(normed, fc1[:, cols])
        hidden = (0.5 * pre * (1.0 + lax.erf(pre * 0.7071067811865476))).astype(BF16)
        acc[...] += dot(hidden, fc2[cols, :])
        return carry

    acc[...] = restored[...].astype(F32)
    lax.fori_loop(0, 4, step, 0)
    pieces = [acc[pl.ds(144 * i, 144), :].astype(BF16).astype(F32) for i in range(4)]
    average = sum(jnp.sum(p, axis=-1, keepdims=True) for p in pieces) / 2048
    pieces = [p - average for p in pieces]
    spread = sum(jnp.sum(p * p, axis=-1, keepdims=True) for p in pieces) / 2048
    scale = lax.rsqrt(spread + 1e-05)
    merged = None
    for i, p in enumerate(pieces):
        term = dot((p * scale).astype(BF16), merge[pl.ds(512 * i, 512), :])
        merged = term if merged is None else merged + term
    return merged


def pack_group(merged, send):
    low = lax.broadcasted_iota(jnp.int32, (72, 128), 1) < 64
    pad = jnp.zeros((8, 128), F32)
    for j in range(8):
        one = merged[0:72, 128 * j : 128 * j + 128]
        two = merged[72:144, 128 * j : 128 * j + 128]
        even = jnp.where(low, one, pltpu.roll(two, 64, 1))
        odd = jnp.where(low, pltpu.roll(one, 64, 1), two)
        send[2 * j] = jnp.concatenate([even, pad], axis=0).astype(BF16)
        send[2 * j + 1] = jnp.concatenate([odd, pad], axis=0).astype(BF16)


def unpack_group(got, out, group):
    for a in range(3):
        lines = jnp.concatenate(
            [got[s].astype(F32)[24 * a : 24 * a + 24, :] for s in range(PEERS)], axis=0
        )
        turned = lines.T
        out[2 * group, a] = turned[0:64, :].astype(BF16)
        out[2 * group + 1, a] = turned[64:128, :].astype(BF16)


def finish_kernel(
    restored, fc1_hbm, fc2_hbm, merge_hbm, out,
    fc1, fc2, merge, acc, send, got, weight_sem, send_sem, recv_sem, own_sem,
):
    loads = [
        pltpu.make_async_copy(src, dst, weight_sem.at[i])
        for i, (src, dst) in enumerate([(fc1_hbm, fc1), (fc2_hbm, fc2), (merge_hbm, merge)])
    ]
    for c in loads:
        c.start()
    me = lax.axis_index("lon")
    barrier = pltpu.get_barrier_semaphore()
    for d in range(1, PEERS):
        pl.semaphore_signal(
            barrier, inc=1, device_id={"lon": lax.rem(me + d, PEERS)}, device_id_type=MESH
        )
    pl.semaphore_wait(barrier, PEERS - 1)
    for c in loads:
        c.wait()
    copies = [[], []]
    for g in range(2):
        merged = finish_group(restored.at[g], fc1, fc2, merge, acc, None)
        pack_group(merged, send.at[g])
        for d in range(1, PEERS):
            to = lax.rem(me + d, PEERS)
            c = pltpu.make_async_remote_copy(
                src_ref=send.at[g, to], dst_ref=got.at[g, me],
                send_sem=send_sem.at[g, d], recv_sem=recv_sem.at[g, d],
                device_id={"lon": to}, device_id_type=MESH,
            )
            c.start()
            copies[g].append(c)
        own = pltpu.make_async_copy(send.at[g, me], got.at[g, me], own_sem.at[g])
        own.start()
        copies[g].append(own)
    for g in range(2):
        for c in copies[g]:
            c.wait()
        unpack_group(got.at[g], out, g)


def finish(restored, fc1_weight, fc2_weight, merge_weight):
    hbm = pl.BlockSpec(memory_space=pl.ANY)
    vmem = pl.BlockSpec(memory_space=pltpu.VMEM)
    dma = pltpu.SemaphoreType.DMA
    return pl.pallas_call(
        finish_kernel,
        out_shape=jax.ShapeDtypeStruct((4, 3, 64, 384), BF16),
        in_specs=[vmem, hbm, hbm, hbm],
        out_specs=vmem,
        scratch_shapes=[
            pltpu.VMEM((512, 2048), BF16),
            pltpu.VMEM((2048, 512), BF16),
            pltpu.VMEM((2048, 1024), BF16),
            pltpu.VMEM((576, 512), F32),
            pltpu.VMEM((2, PEERS, 80, 128), BF16),
            pltpu.VMEM((2, PEERS, 80, 128), BF16),
            dma((3,)),
            dma((2, PEERS)),
            dma((2, PEERS)),
            dma((2,)),
        ],
        compiler_params=pltpu.CompilerParams(
            collective_id=0, has_side_effects=True, vmem_limit_bytes=56 * 1024 * 1024
        ),
        name="finish",
    )(restored, fc1_weight, fc2_weight, merge_weight)


def body(tokens, band_ids, qkv_weight, proj_weight, fc1_weight, fc2_weight, merge_weight):
    lat_rim = WIN_LAT // 2
    lon_rim = WIN_LON // 2
    rows_dev = tokens.shape[1]
    below_rim = shifted_2(tokens[:, :lat_rim], "lat", -1)
    moved_rows = jnp.concatenate([tokens[:, lat_rim:], below_rim], axis=1)
    beside = shifted_2(moved_rows[:, :, :lon_rim], "lon", -1)
    shifted = jnp.concatenate([moved_rows[:, :, lon_rim:], beside], axis=2)
    lat_total = lax.axis_size("lat") * rows_dev
    offset = (lax.axis_index("lat") * rows_dev + lat_rim) % lat_total
    band_rows = lax.dynamic_slice_in_dim(jnp.concatenate([band_ids, band_ids]), offset, rows_dev)
    updated = window_attention(shifted, band_rows, qkv_weight, proj_weight)
    returned = shifted_2(updated[:, -lat_rim:], "lat", 1)
    restored = jnp.concatenate([returned, updated[:, :-lat_rim]], axis=1)
    returned_cols = shifted_2(restored[:, :, -lon_rim:], "lon", 1)
    restored = jnp.concatenate([returned_cols, restored[:, :, :-lon_rim]], axis=2)
    ordered = restored.reshape(2, 2, 3, 2, 24, 2, 512).transpose(0, 5, 3, 1, 2, 4, 6)
    return finish(ordered.reshape(2, 576, 512), fc1_weight, fc2_weight, merge_weight)


def solution(mesh):
    placed = (P(None, "lat", "lon", None), P(), P(), P(), P(), P(), P())
    return jax.shard_map(
        body, mesh=mesh, in_specs=placed, out_specs=P(None, "lat", "lon", None), check_vma=False
    )
```

```python
import jax
import jax.numpy as jnp
import numpy as np
from jax import lax
from jax.experimental import pallas as pl
from jax.experimental.pallas import tpu as pltpu
from jax.sharding import PartitionSpec as P

MESH = pl.DeviceIdType.MESH
BF16 = jnp.bfloat16
F32 = jnp.float32
PEERS = 16
LAT = 8
WIDTH = 512
NEVER = -1e30


def unit_row(half, unit):
    return unit if half == 0 else 5 - unit


def one_hots():
    first = np.zeros((80, 576), np.float32)
    window = np.zeros((576, 576), np.float32)
    window_edge = np.zeros((576, 80), np.float32)
    back = np.zeros((80, 144), np.float32)
    merge = np.zeros((576, 576), np.float32)
    merge_edge = np.zeros((576, 80), np.float32)

    def home(level, row, col):
        return (level * 6 + row) * 48 + col

    def merged(level, row, col):
        return (((col % 2) * 2 + row % 2) * 2 + level) * 72 + (row // 2) * 24 + col // 2

    for half in range(2):
        for unit in range(3):
            row = unit_row(half, unit)
            for level in range(2):
                for col in range(6):
                    edge = ((half * 3 + unit) * 2 + level) * 6 + col
                    first[edge, home(level, row, col)] = 1
                    back[edge, half * 72 + (unit * 2 + level) * 12 + 6 + col] = 1
                    merge_edge[merged(level, row, col), edge] = 1
                for win in range(4):
                    for col in range(12):
                        place = ((half * 4 + win) * 3 + unit) * 24 + level * 12 + col
                        at = win * 12 + 6 + col
                        if at < 48:
                            window[place, home(level, row, at)] = 1
                            merge[merged(level, row, at), place] = 1
                        else:
                            edge = ((half * 3 + unit) * 2 + level) * 6 + at - 48
                            window_edge[place, edge] = 1
    return [first, window, window_edge, back, merge, merge_edge]


ONE_HOTS = one_hots()


def dot(a, b):
    return jnp.dot(a, b, preferred_element_type=F32)


def layer_norm(values):
    average = jnp.mean(values, axis=-1, keepdims=True)
    centred = values - average
    spread = jnp.mean(centred * centred, axis=-1, keepdims=True)
    return centred * lax.rsqrt(spread + 1e-05)


def attend(block, query_at, queries, keys, bias):
    low = lax.broadcasted_iota(jnp.int32, (queries, 128), 1) < 64
    ones = jnp.ones((keys, 128), BF16)
    result = []
    for pair in range(4):
        at = 128 * pair
        query = block[pl.ds(query_at, queries), pl.ds(at, 128)] * 0.125
        query = jnp.concatenate([jnp.where(low, query, 0.0), jnp.where(low, 0.0, query)], axis=0)
        key = block[pl.ds(0, keys), pl.ds(512 + at, 128)].astype(BF16)
        value = block[pl.ds(0, keys), pl.ds(1024 + at, 128)].astype(BF16)
        scores = lax.dot_general(
            query.astype(BF16), key, (((1,), (1,)), ((), ())), preferred_element_type=F32
        )
        scores = scores + bias
        weights = jnp.exp(scores - jnp.max(scores, axis=-1, keepdims=True)).astype(BF16)
        sums = dot(weights, jnp.concatenate([value, ones], axis=1))
        mixed = sums[:, 0:128] / sums[:, 128:256]
        result.append(jnp.where(low, mixed[0:queries], mixed[queries:]))
    return result


def finish_group(restored, fc1, fc2, merge, acc):
    base = restored.astype(F32)
    normed = layer_norm(base).astype(BF16)
    part = 512

    def step(i, carry):
        cols = pl.ds(pl.multiple_of(i * part, part), part)
        pre = dot(normed, fc1[:, cols])
        hidden = (0.5 * pre * (1.0 + lax.erf(pre * 0.7071067811865476))).astype(BF16)
        acc[...] += dot(hidden, fc2[cols, :])
        return carry

    acc[...] = base
    lax.fori_loop(0, 4, step, 0)
    pieces = [acc[pl.ds(144 * i, 144), :].astype(BF16).astype(F32) for i in range(4)]
    average = sum(jnp.sum(p, axis=-1, keepdims=True) for p in pieces) / 2048
    pieces = [p - average for p in pieces]
    spread = sum(jnp.sum(p * p, axis=-1, keepdims=True) for p in pieces) / 2048
    scale = lax.rsqrt(spread + 1e-05)
    merged = None
    for i, p in enumerate(pieces):
        term = dot((p * scale).astype(BF16), merge[pl.ds(512 * i, 512), :])
        merged = term if merged is None else merged + term
    return merged


def pack_group(merged, send):
    low = lax.broadcasted_iota(jnp.int32, (72, 128), 1) < 64
    pad = jnp.zeros((8, 128), F32)
    for j in range(8):
        one = merged[0:72, 128 * j : 128 * j + 128]
        two = merged[72:144, 128 * j : 128 * j + 128]
        even = jnp.where(low, one, pltpu.roll(two, 64, 1))
        odd = jnp.where(low, pltpu.roll(one, 64, 1), two)
        send[2 * j] = jnp.concatenate([even, pad], axis=0).astype(BF16)
        send[2 * j + 1] = jnp.concatenate([odd, pad], axis=0).astype(BF16)


def unpack_group(got, out, group):
    for a in range(3):
        lines = jnp.concatenate(
            [got[s].astype(F32)[24 * a : 24 * a + 24, :] for s in range(PEERS)], axis=0
        )
        turned = lines.T
        out[2 * group, a] = turned[0:64, :].astype(BF16)
        out[2 * group + 1, a] = turned[64:128, :].astype(BF16)


def kernel(
    tokens_hbm, first_hbm, window_hbm, window_edge_hbm, back_hbm, merge_order_hbm, merge_edge_hbm,
    qkv_hbm, proj_hbm, fc1_hbm, fc2_hbm, merge_hbm, bias_own, bias_rim, flags,
    out,
    tokens, first, window, window_edge, back, merge_order, merge_edge,
    qkv, proj, fc1, fc2, merge,
    edge_out, edge_in, ordered, rim_out, rim_in, far_out, far_in, packed, mixed, updated,
    back_out, back_in, acc, send, got,
    token_sem, load_sem, edge_sem, rim_sem, far_sem, back_sem, send_sem, recv_sem, own_sem,
):
    sources = [
        first_hbm, window_hbm, window_edge_hbm, qkv_hbm, proj_hbm, back_hbm, merge_order_hbm,
        merge_edge_hbm, fc1_hbm, fc2_hbm, merge_hbm,
    ]
    places = [
        first, window, window_edge, qkv, proj, back, merge_order, merge_edge, fc1, fc2, merge,
    ]
    token_loads = [
        pltpu.make_async_copy(tokens_hbm.at[pl.ds(576 * g, 576)], tokens.at[g], token_sem.at[g])
        for g in range(2)
    ]
    loads = [
        pltpu.make_async_copy(src, dst, load_sem.at[i])
        for i, (src, dst) in enumerate(zip(sources, places))
    ]
    token_loads[0].start()
    loads[0].start()
    token_loads[1].start()
    for load in loads[1:]:
        load.start()

    lat = lax.axis_index("lat")
    lon = lax.axis_index("lon")
    up = {"lat": lax.rem(lat + LAT - 1, LAT)}
    down = {"lat": lax.rem(lat + 1, LAT)}
    west = {"lon": lax.rem(lon + PEERS - 1, PEERS)}
    east = {"lon": lax.rem(lon + 1, PEERS)}
    barrier = pltpu.get_barrier_semaphore()
    for d in range(1, PEERS):
        pl.semaphore_signal(
            barrier, inc=1, device_id={"lon": lax.rem(lon + d, PEERS)}, device_id_type=MESH
        )
    for to in (up, down):
        pl.semaphore_signal(barrier, inc=1, device_id=to, device_id_type=MESH)
    pl.semaphore_wait(barrier, PEERS + 1)

    def remote(src, dst, sems, where, to):
        copy = pltpu.make_async_remote_copy(
            src_ref=src, dst_ref=dst, send_sem=sems.at[(0,) + where], recv_sem=sems.at[(1,) + where],
            device_id=to, device_id_type=MESH,
        )
        copy.start()
        return copy

    edges = []
    for g in range(2):
        token_loads[g].wait()
        if g == 0:
            loads[0].wait()
        edge_out[g] = dot(first[...], tokens[g]).astype(BF16)
        edges.append(remote(edge_out.at[g], edge_in.at[g], edge_sem, (g,), west))
    for load in loads[1:3]:
        load.wait()
    rims = []
    for g in range(2):
        inner = dot(window[...], tokens[g])
        edges[g].wait_recv()
        placed = inner + dot(window_edge[...], edge_in[g])
        ordered[g] = placed.astype(BF16)
        for half in range(2):
            rim_out[g, half] = jnp.concatenate(
                [placed[288 * half + 72 * w : 288 * half + 72 * w + 24] for w in range(4)], axis=0
            ).astype(BF16)
            far_out[g, half] = jnp.concatenate(
                [placed[288 * half + 72 * w + 24 : 288 * half + 72 * w + 48] for w in range(4)], axis=0
            ).astype(BF16)
            rims.append(
                remote(rim_out.at[g, half], rim_in.at[g, 1 - half], rim_sem, (g, half), (up, down)[half])
            )
    loads[3].wait()
    for g in range(2):
        normed = layer_norm(ordered[g].astype(F32)).astype(BF16)
        for part in range(3):
            cols = pl.ds(512 * part, 512)
            result = dot(normed, qkv[:, cols])
            for k in range(8):
                packed[g, k, pl.ds(0, 72), cols] = result[72 * k : 72 * k + 72]
        for k in range(8):
            packed[g, k, pl.ds(120, 8), :] = jnp.zeros((8, 1536), F32)
    fars = []
    for g in range(2):
        for half in range(2):
            rims[2 * g + half].wait_recv()
        rim = rim_in[g].reshape(192, WIDTH)
        normed = layer_norm(rim.astype(F32)).astype(BF16)
        for part in range(3):
            cols = pl.ds(512 * part, 512)
            result = dot(normed, qkv[:, cols])
            for k in range(8):
                packed[g, k, pl.ds(72, 24), cols] = result[24 * k : 24 * k + 24]

        def rim_step(k, carry, g=g):
            parts = attend(packed.at[g, k], 72, 24, 96, bias_rim[k // 4])
            for pair in range(4):
                mixed[g, pl.ds(pl.multiple_of(k * 72, 8), 24), pl.ds(128 * pair, 128)] = parts[pair]
            return carry

        lax.fori_loop(0, 8, rim_step, 0)
        for half in range(2):
            seen = jnp.concatenate(
                [mixed[g, pl.ds(288 * half + 72 * w, 24), :] for w in range(4)], axis=0
            )
            far_out[g, half] = jnp.where(
                flags[pl.ds(half, 1), :] > 0, seen, far_out[g, half].astype(F32)
            ).astype(BF16)
            fars.append(
                remote(far_out.at[g, half], far_in.at[g, 1 - half], far_sem, (g, half), (up, down)[half])
            )
    loads[4].wait()
    loads[5].wait()
    copies = []
    backs = []
    for g in range(2):
        for half in range(2):
            fars[2 * g + half].wait_recv()
        far = far_in[g].reshape(192, WIDTH)
        normed = layer_norm(far.astype(F32)).astype(BF16)
        for part in range(1, 3):
            cols = pl.ds(512 * part, 512)
            result = dot(normed, qkv[:, cols])
            for k in range(8):
                packed[g, k, pl.ds(96, 24), cols] = result[24 * k : 24 * k + 24]

        def own_step(k, carry, g=g):
            parts = attend(packed.at[g, k], 0, 72, 128, bias_own[k // 4])
            for pair in range(4):
                mixed[g, pl.ds(pl.multiple_of(k * 72, 8), 72), pl.ds(128 * pair, 128)] = parts[pair]
            return carry

        lax.fori_loop(0, 8, own_step, 0)
        for half in range(2):
            final = far_in[g, half].astype(F32)
            for w in range(4):
                rows = pl.ds(288 * half + 72 * w, 24)
                mixed[g, rows, :] = jnp.where(
                    flags[pl.ds(2 + half, 1), :] > 0, final[24 * w : 24 * w + 24], mixed[g, rows, :]
                )
        fresh = ordered[g].astype(F32) + dot(mixed[g].astype(BF16), proj[...])
        updated[g] = fresh.astype(BF16)
        rim = jnp.concatenate([fresh[216:288], fresh[504:576]], axis=0).astype(BF16)
        back_out[g] = dot(back[...], rim).astype(BF16)
        backs.append(remote(back_out.at[g], back_in.at[g], back_sem, (g,), east))
        if g == 0:
            for load in loads[6:]:
                load.wait()
        inner = dot(merge_order[...], updated[g])
        backs[g].wait_recv()
        restored = (inner + dot(merge_edge[...], back_in[g])).astype(BF16)
        merged = finish_group(restored, fc1, fc2, merge, acc)
        pack_group(merged, send.at[g])
        for d in range(1, PEERS):
            to = lax.rem(lon + d, PEERS)
            copy = pltpu.make_async_remote_copy(
                src_ref=send.at[g, to], dst_ref=got.at[g, lon],
                send_sem=send_sem.at[g, d], recv_sem=recv_sem.at[g, d],
                device_id={"lon": to}, device_id_type=MESH,
            )
            copy.start()
            copies.append(copy)
        own = pltpu.make_async_copy(send.at[g, lon], got.at[g, lon], own_sem.at[g])
        own.start()
        copies.append(own)
    for g in range(2):
        for copy in copies[16 * g : 16 * g + 16]:
            copy.wait()
        unpack_group(got.at[g], out, g)
    for copy in edges + rims + fars + backs:
        copy.wait_send()


def body(tokens, band_ids, qkv_weight, proj_weight, fc1_weight, fc2_weight, merge_weight):
    constants = [jnp.asarray(m, BF16) for m in ONE_HOTS]
    start = lax.axis_index("lat") * 6
    around = lax.dynamic_slice_in_dim(jnp.concatenate([band_ids[45:], band_ids, band_ids[:3]]), start, 12)
    bias_own, bias_rim, edge_out, edge_in = [], [], [], []
    for half in range(2):
        units = [unit_row(half, u) for u in range(3)] + ([-1, -2, -3] if half == 0 else [6, 7, 8])
        band = [around[u + 3] for u in units]
        key = jnp.concatenate([jnp.stack(band[:5]).repeat(24), jnp.full((8,), -1, jnp.int32)])
        bias = jnp.where(key[:, None] == key[None, :], 0.0, NEVER).astype(F32)
        bias_own.append(jnp.concatenate([bias[:72], bias[:72]], axis=0))
        bias_rim.append(jnp.concatenate([bias[72:96, :96], bias[72:96, :96]], axis=0))
        edge_out.append(band[2] == band[3])
        edge_in.append(band[0] == band[5])
    flags = jnp.broadcast_to(jnp.stack(edge_out + edge_in)[:, None].astype(F32), (4, WIDTH))
    hbm = pl.BlockSpec(memory_space=pl.ANY)
    vmem = pl.BlockSpec(memory_space=pltpu.VMEM)
    dma = pltpu.SemaphoreType.DMA
    return pl.pallas_call(
        kernel,
        out_shape=jax.ShapeDtypeStruct((4, 3, 64, 384), BF16),
        in_specs=[hbm] * 12 + [vmem] * 3,
        out_specs=vmem,
        scratch_shapes=[
            pltpu.VMEM((2, 576, WIDTH), BF16),
            pltpu.VMEM((80, 576), BF16),
            pltpu.VMEM((576, 576), BF16),
            pltpu.VMEM((576, 80), BF16),
            pltpu.VMEM((80, 144), BF16),
            pltpu.VMEM((576, 576), BF16),
            pltpu.VMEM((576, 80), BF16),
            pltpu.VMEM((512, 1536), BF16),
            pltpu.VMEM((512, 512), BF16),
            pltpu.VMEM((512, 2048), BF16),
            pltpu.VMEM((2048, 512), BF16),
            pltpu.VMEM((2048, 1024), BF16),
            pltpu.VMEM((2, 80, WIDTH), BF16),
            pltpu.VMEM((2, 80, WIDTH), BF16),
            pltpu.VMEM((2, 576, WIDTH), BF16),
            pltpu.VMEM((2, 2, 96, WIDTH), BF16),
            pltpu.VMEM((2, 2, 96, WIDTH), BF16),
            pltpu.VMEM((2, 2, 96, WIDTH), BF16),
            pltpu.VMEM((2, 2, 96, WIDTH), BF16),
            pltpu.VMEM((2, 8, 128, 1536), F32),
            pltpu.VMEM((2, 576, WIDTH), F32),
            pltpu.VMEM((2, 576, WIDTH), BF16),
            pltpu.VMEM((2, 80, WIDTH), BF16),
            pltpu.VMEM((2, 80, WIDTH), BF16),
            pltpu.VMEM((576, WIDTH), F32),
            pltpu.VMEM((2, PEERS, 80, 128), BF16),
            pltpu.VMEM((2, PEERS, 80, 128), BF16),
            dma((2,)),
            dma((11,)),
            dma((2, 2)),
            dma((2, 2, 2)),
            dma((2, 2, 2)),
            dma((2, 2)),
            dma((2, PEERS)),
            dma((2, PEERS)),
            dma((2,)),
        ],
        compiler_params=pltpu.CompilerParams(
            collective_id=0, has_side_effects=True, vmem_limit_bytes=56 * 1024 * 1024
        ),
        name="layer",
    )(
        tokens.reshape(4 * 6 * 48, WIDTH), *constants,
        qkv_weight, proj_weight, fc1_weight, fc2_weight, merge_weight,
        jnp.stack(bias_own), jnp.stack(bias_rim), flags,
    )


def solution(mesh):
    placed = (P(None, "lat", "lon", None), P(), P(), P(), P(), P(), P())
    return jax.shard_map(
        body, mesh=mesh, in_specs=placed, out_specs=P(None, "lat", "lon", None), check_vma=False
    )
```

```python
import jax
import jax.numpy as jnp
from jax import lax
from jax.experimental import pallas as pl
from jax.experimental.pallas import tpu as pltpu
from jax.sharding import PartitionSpec as P

MESH = pl.DeviceIdType.MESH
BF16 = jnp.bfloat16
F32 = jnp.float32
PEERS = 16
LAT = 8
WIDTH = 512
NEVER = -1e30


def unit_row(half, unit):
    return unit if half == 0 else 5 - unit


def split(index, size):
    whole = jnp.floor((index + 0.5) * (1.0 / size))
    return whole, index - whole * size


def one_hot(picks, width):
    lane = lax.broadcasted_iota(jnp.int32, picks.shape, 1).astype(F32)
    tiles = [jnp.where(lane + at == picks, 1.0, 0.0) for at in range(0, width, 128)]
    return jnp.concatenate(tiles, axis=1)[:, 0:width].astype(BF16)


def index_of(rows):
    return lax.broadcasted_iota(jnp.int32, (rows, 128), 0).astype(F32)


def edge_picks():
    index = index_of(80)
    half, rest = split(index, 36)
    unit, rest = split(rest, 12)
    level, col = split(rest, 6)
    row = unit + half * (5 - 2 * unit)
    real = index < 72
    first = jnp.where(real, (level * 6 + row) * 48 + col, -1.0)
    back = jnp.where(real, half * 72 + (unit * 2 + level) * 12 + 6 + col, -1.0)
    return first, back


def window_picks():
    half, rest = split(index_of(576), 288)
    win, rest = split(rest, 72)
    unit, rest = split(rest, 24)
    level, col = split(rest, 12)
    row = unit + half * (5 - 2 * unit)
    at = win * 12 + 6 + col
    here = at < 48
    inner = jnp.where(here, (level * 6 + row) * 48 + at, -1.0)
    edge = jnp.where(here, -1.0, ((half * 3 + unit) * 2 + level) * 6 + at - 48)
    return inner, edge


def merge_picks():
    parity, rest = split(index_of(576), 144)
    col_parity, row_parity = split(parity, 2)
    level, rest = split(rest, 72)
    a, b = split(rest, 24)
    row = 2 * a + row_parity
    col = 2 * b + col_parity
    half = jnp.where(row > 2.5, 1.0, 0.0)
    unit = row + half * (5 - 2 * row)
    win, at = split(col - 6, 12)
    here = col > 5.5
    inner = jnp.where(here, ((half * 4 + win) * 3 + unit) * 24 + level * 12 + at, -1.0)
    edge = jnp.where(here, -1.0, ((half * 3 + unit) * 2 + level) * 6 + col)
    return inner, edge


def dot(a, b):
    return jnp.dot(a, b, preferred_element_type=F32)


def layer_norm(values):
    average = jnp.mean(values, axis=-1, keepdims=True)
    centred = values - average
    spread = jnp.mean(centred * centred, axis=-1, keepdims=True)
    return centred * lax.rsqrt(spread + 1e-05)


def attend(block, query_at, bias):
    head = lax.broadcasted_iota(jnp.int32, (48, 256), 1) // 64
    result = []
    for quad in range(2):
        at = 256 * quad
        query = block[pl.ds(query_at, 48), pl.ds(at, 256)] * 0.125
        query = jnp.concatenate([jnp.where(head == h, query, 0.0) for h in range(4)], axis=0)
        key = block[:, pl.ds(512 + at, 256)].astype(BF16)
        value = block[:, pl.ds(1024 + at, 256)].astype(BF16)
        scores = lax.dot_general(
            query.astype(BF16), key, (((1,), (1,)), ((), ())), preferred_element_type=F32
        )
        scores = scores + bias
        weights = jnp.exp(scores - jnp.max(scores, axis=-1, keepdims=True))
        total = jnp.sum(weights, axis=-1, keepdims=True)
        mixed = dot(weights.astype(BF16), value) / total
        picked = mixed[0:48]
        for h in range(1, 4):
            picked = jnp.where(head == h, mixed[48 * h : 48 * h + 48], picked)
        result.append(picked)
    return result


def band_biases(band_ids, lat, bias_own, bias_rim):
    seen, final = [], []
    for half in range(2):
        units = [unit_row(half, u) for u in range(3)] + ([-1, -2, -3] if half == 0 else [6, 7, 8])
        band = [band_ids[lax.rem(lat * 6 + u + 48, 48)] for u in units]

        def band_of(shape, dim):
            unit = lax.broadcasted_iota(jnp.int32, shape, dim) // 24
            held = jnp.full(shape, -1, jnp.int32)
            for u in range(5):
                held = jnp.where(unit == u, band[u], held)
            return held

        bias = jnp.where(band_of((96, 128), 0) == band_of((96, 128), 1), 0.0, NEVER)
        near = lax.broadcasted_iota(jnp.int32, (48, 128), 1) < 96
        for head in range(4):
            bias_own[half, pl.ds(48 * head, 48), :] = bias[0:48]
            bias_rim[half, pl.ds(48 * head, 48), :] = jnp.where(near, bias[48:96], NEVER)
        seen.append(jnp.full((1, WIDTH), band[2], jnp.int32) == band[3])
        final.append(jnp.full((1, WIDTH), band[0], jnp.int32) == band[5])
    return seen, final


def finish_group(restored, fc1, fc2, merge, acc):
    base = restored.astype(F32)
    normed = layer_norm(base).astype(BF16)
    hidden = []
    for i in range(4):
        pre = dot(normed, fc1[:, pl.ds(512 * i, 512)])
        hidden.append((0.5 * pre * (1.0 + lax.erf(pre * 0.7071067811865476))).astype(BF16))
    acc[...] = base + dot(jnp.concatenate(hidden, axis=1), fc2[...])
    pieces = [acc[pl.ds(144 * i, 144), :].astype(BF16).astype(F32) for i in range(4)]
    average = sum(jnp.sum(p, axis=-1, keepdims=True) for p in pieces) / 2048
    pieces = [p - average for p in pieces]
    spread = sum(jnp.sum(p * p, axis=-1, keepdims=True) for p in pieces) / 2048
    scale = lax.rsqrt(spread + 1e-05)
    merged = None
    for i, p in enumerate(pieces):
        term = dot((p * scale).astype(BF16), merge[pl.ds(512 * i, 512), :])
        merged = term if merged is None else merged + term
    return merged


def pack_group(merged, send):
    low = lax.broadcasted_iota(jnp.int32, (72, 128), 1) < 64
    pad = jnp.zeros((8, 128), F32)
    for j in range(8):
        one = merged[0:72, 128 * j : 128 * j + 128]
        two = merged[72:144, 128 * j : 128 * j + 128]
        even = jnp.where(low, one, pltpu.roll(two, 64, 1))
        odd = jnp.where(low, pltpu.roll(one, 64, 1), two)
        send[2 * j] = jnp.concatenate([even, pad], axis=0).astype(BF16)
        send[2 * j + 1] = jnp.concatenate([odd, pad], axis=0).astype(BF16)


def unpack_group(got, out, group):
    for a in range(3):
        lines = jnp.concatenate(
            [got[s].astype(F32)[24 * a : 24 * a + 24, :] for s in range(PEERS)], axis=0
        )
        turned = lines.T
        out[2 * group, a] = turned[0:64, :].astype(BF16)
        out[2 * group + 1, a] = turned[64:128, :].astype(BF16)


def kernel(
    tokens_hbm, qkv_hbm, proj_hbm, fc1_hbm, fc2_hbm, merge_hbm, band_ids,
    out,
    tokens, first, window, window_edge, back, merge_order, merge_edge,
    qkv, proj, fc1, fc2, merge,
    edge_out, edge_in, ordered, rim_out, rim_in, far_out, far_in, packed, mixed, updated,
    back_out, back_in, acc, send, got, bias_own, bias_rim, rim_mixed,
    token_sem, load_sem, edge_sem, rim_sem, far_sem, back_sem, send_sem, recv_sem, own_sem,
):
    sources = [qkv_hbm, proj_hbm, fc1_hbm, fc2_hbm, merge_hbm]
    places = [qkv, proj, fc1, fc2, merge]
    token_loads = [
        pltpu.make_async_copy(tokens_hbm.at[pl.ds(576 * g, 576)], tokens.at[g], token_sem.at[g])
        for g in range(2)
    ]
    loads = [
        pltpu.make_async_copy(src, dst, load_sem.at[i])
        for i, (src, dst) in enumerate(zip(sources, places))
    ]
    for load in token_loads + loads:
        load.start()

    lat = lax.axis_index("lat")
    lon = lax.axis_index("lon")
    up = {"lat": lax.rem(lat + LAT - 1, LAT)}
    down = {"lat": lax.rem(lat + 1, LAT)}
    west = {"lon": lax.rem(lon + PEERS - 1, PEERS)}
    east = {"lon": lax.rem(lon + 1, PEERS)}
    barrier = pltpu.get_barrier_semaphore()
    for d in range(1, PEERS):
        pl.semaphore_signal(
            barrier, inc=1, device_id={"lon": lax.rem(lon + d, PEERS)}, device_id_type=MESH
        )
    for to in (up, down):
        pl.semaphore_signal(barrier, inc=1, device_id=to, device_id_type=MESH)
    picks, back_picks = edge_picks()
    first[...] = one_hot(picks, 576)
    back[...] = one_hot(back_picks, 144)
    picks, far_picks = window_picks()
    window[...] = one_hot(picks, 576)
    window_edge[...] = one_hot(far_picks, 80)
    pl.semaphore_wait(barrier, PEERS + 1)

    def remote(src, dst, sems, where, to):
        copy = pltpu.make_async_remote_copy(
            src_ref=src, dst_ref=dst, send_sem=sems.at[(0,) + where], recv_sem=sems.at[(1,) + where],
            device_id=to, device_id_type=MESH,
        )
        copy.start()
        return copy

    edges = []
    for g in range(2):
        token_loads[g].wait()
        edge_out[g] = dot(first[...], tokens[g]).astype(BF16)
        edges.append(remote(edge_out.at[g], edge_in.at[g], edge_sem, (g,), west))
    rims = []
    for g in range(2):
        inner = dot(window[...], tokens[g])
        edges[g].wait_recv()
        placed = inner + dot(window_edge[...], edge_in[g])
        ordered[g] = placed.astype(BF16)
        for half in range(2):
            rim_out[g, half] = jnp.concatenate(
                [placed[288 * half + 72 * w : 288 * half + 72 * w + 24] for w in range(4)], axis=0
            ).astype(BF16)
            far_out[g, half] = jnp.concatenate(
                [placed[288 * half + 72 * w + 24 : 288 * half + 72 * w + 48] for w in range(4)], axis=0
            ).astype(BF16)
            rims.append(
                remote(rim_out.at[g, half], rim_in.at[g, 1 - half], rim_sem, (g, half), (up, down)[half])
            )
    picks, far_picks = merge_picks()
    merge_order[...] = one_hot(picks, 576)
    merge_edge[...] = one_hot(far_picks, 80)
    edge_seen, edge_final = band_biases(band_ids, lat, bias_own, bias_rim)
    loads[0].wait()
    for g in range(2):
        normed = layer_norm(ordered[g].astype(F32)).astype(BF16)
        for part in range(3):
            cols = pl.ds(512 * part, 512)
            result = dot(normed, qkv[:, cols])
            for k in range(8):
                packed[g, k, pl.ds(0, 72), cols] = result[72 * k : 72 * k + 72]
        for k in range(8):
            packed[g, k, pl.ds(96, 32), :] = jnp.zeros((32, 1536), F32)
    fars = []
    for g in range(2):
        for half in range(2):
            rims[2 * g + half].wait_recv()
        rim = rim_in[g].reshape(192, WIDTH)
        normed = layer_norm(rim.astype(F32)).astype(BF16)
        for part in range(3):
            cols = pl.ds(512 * part, 512)
            result = dot(normed, qkv[:, cols])
            for k in range(8):
                packed[g, k, pl.ds(72, 24), cols] = result[24 * k : 24 * k + 24]

        for k in range(8):
            parts = attend(packed.at[g, k], 48, bias_rim[k // 4])
            for quad in range(2):
                cols = pl.ds(256 * quad, 256)
                mixed[g, pl.ds(72 * k + 48, 24), cols] = parts[quad][0:24]
                rim_mixed[g, pl.ds(24 * k, 24), cols] = parts[quad][24:48]
        for half in range(2):
            seen = rim_mixed[g, pl.ds(96 * half, 96), :]
            far_out[g, half] = jnp.where(
                edge_seen[half], seen, far_out[g, half].astype(F32)
            ).astype(BF16)
            fars.append(
                remote(far_out.at[g, half], far_in.at[g, 1 - half], far_sem, (g, half), (up, down)[half])
            )
    loads[1].wait()
    copies = []
    backs = []
    for g in range(2):
        for half in range(2):
            fars[2 * g + half].wait_recv()
        far = far_in[g].reshape(192, WIDTH)
        normed = layer_norm(far.astype(F32)).astype(BF16)
        for part in range(1, 3):
            cols = pl.ds(512 * part, 512)
            result = dot(normed, qkv[:, cols])
            for k in range(8):
                packed[g, k, pl.ds(96, 24), cols] = result[24 * k : 24 * k + 24]

        for k in range(8):
            parts = attend(packed.at[g, k], 0, bias_own[k // 4])
            for quad in range(2):
                mixed[g, pl.ds(72 * k, 48), pl.ds(256 * quad, 256)] = parts[quad]
        for half in range(2):
            final = far_in[g, half].astype(F32)
            for w in range(4):
                rows = pl.ds(288 * half + 72 * w, 24)
                mixed[g, rows, :] = jnp.where(
                    edge_final[half], final[24 * w : 24 * w + 24], mixed[g, rows, :]
                )
        fresh = ordered[g].astype(F32) + dot(mixed[g].astype(BF16), proj[...])
        updated[g] = fresh.astype(BF16)
        rim = jnp.concatenate([fresh[216:288], fresh[504:576]], axis=0).astype(BF16)
        back_out[g] = dot(back[...], rim).astype(BF16)
        backs.append(remote(back_out.at[g], back_in.at[g], back_sem, (g,), east))
        if g == 0:
            for load in loads[2:]:
                load.wait()
        inner = dot(merge_order[...], updated[g])
        backs[g].wait_recv()
        restored = (inner + dot(merge_edge[...], back_in[g])).astype(BF16)
        merged = finish_group(restored, fc1, fc2, merge, acc)
        pack_group(merged, send.at[g])
        for d in range(1, PEERS):
            to = lax.rem(lon + d, PEERS)
            copy = pltpu.make_async_remote_copy(
                src_ref=send.at[g, to], dst_ref=got.at[g, lon],
                send_sem=send_sem.at[g, d], recv_sem=recv_sem.at[g, d],
                device_id={"lon": to}, device_id_type=MESH,
            )
            copy.start()
            copies.append(copy)
        own = pltpu.make_async_copy(send.at[g, lon], got.at[g, lon], own_sem.at[g])
        own.start()
        copies.append(own)
    for g in range(2):
        for copy in copies[16 * g : 16 * g + 16]:
            copy.wait()
        unpack_group(got.at[g], out, g)
    for copy in edges + rims + fars + backs:
        copy.wait_send()


def body(tokens, band_ids, qkv_weight, proj_weight, fc1_weight, fc2_weight, merge_weight):
    hbm = pl.BlockSpec(memory_space=pl.ANY)
    vmem = pl.BlockSpec(memory_space=pltpu.VMEM)
    dma = pltpu.SemaphoreType.DMA
    return pl.pallas_call(
        kernel,
        out_shape=jax.ShapeDtypeStruct((4, 3, 64, 384), BF16),
        in_specs=[hbm] * 6 + [pl.BlockSpec(memory_space=pltpu.SMEM)],
        out_specs=vmem,
        scratch_shapes=[
            pltpu.VMEM((2, 576, WIDTH), BF16),
            pltpu.VMEM((80, 576), BF16),
            pltpu.VMEM((576, 576), BF16),
            pltpu.VMEM((576, 80), BF16),
            pltpu.VMEM((80, 144), BF16),
            pltpu.VMEM((576, 576), BF16),
            pltpu.VMEM((576, 80), BF16),
            pltpu.VMEM((512, 1536), BF16),
            pltpu.VMEM((512, 512), BF16),
            pltpu.VMEM((512, 2048), BF16),
            pltpu.VMEM((2048, 512), BF16),
            pltpu.VMEM((2048, 1024), BF16),
            pltpu.VMEM((2, 80, WIDTH), BF16),
            pltpu.VMEM((2, 80, WIDTH), BF16),
            pltpu.VMEM((2, 576, WIDTH), BF16),
            pltpu.VMEM((2, 2, 96, WIDTH), BF16),
            pltpu.VMEM((2, 2, 96, WIDTH), BF16),
            pltpu.VMEM((2, 2, 96, WIDTH), BF16),
            pltpu.VMEM((2, 2, 96, WIDTH), BF16),
            pltpu.VMEM((2, 8, 128, 1536), F32),
            pltpu.VMEM((2, 576, WIDTH), F32),
            pltpu.VMEM((2, 576, WIDTH), BF16),
            pltpu.VMEM((2, 80, WIDTH), BF16),
            pltpu.VMEM((2, 80, WIDTH), BF16),
            pltpu.VMEM((576, WIDTH), F32),
            pltpu.VMEM((2, PEERS, 80, 128), BF16),
            pltpu.VMEM((2, PEERS, 80, 128), BF16),
            pltpu.VMEM((2, 192, 128), F32),
            pltpu.VMEM((2, 192, 128), F32),
            pltpu.VMEM((2, 192, WIDTH), F32),
            dma((2,)),
            dma((5,)),
            dma((2, 2)),
            dma((2, 2, 2)),
            dma((2, 2, 2)),
            dma((2, 2)),
            dma((2, PEERS)),
            dma((2, PEERS)),
            dma((2,)),
        ],
        compiler_params=pltpu.CompilerParams(
            collective_id=0, has_side_effects=True, vmem_limit_bytes=56 * 1024 * 1024
        ),
        name="layer",
    )(
        tokens.reshape(4 * 6 * 48, WIDTH),
        qkv_weight, proj_weight, fc1_weight, fc2_weight, merge_weight, band_ids,
    )


def solution(mesh):
    placed = (P(None, "lat", "lon", None), P(), P(), P(), P(), P(), P())
    return jax.shard_map(
        body, mesh=mesh, in_specs=placed, out_specs=P(None, "lat", "lon", None), check_vma=False
    )
```

```python
import jax
import jax.numpy as jnp
from jax import lax
from jax.experimental import pallas as pl
from jax.experimental.pallas import tpu as pltpu
from jax.sharding import PartitionSpec as P

MESH = pl.DeviceIdType.MESH
BF16 = jnp.bfloat16
F32 = jnp.float32
PEERS = 16
LAT = 8
WIDTH = 512
NEVER = -1e30


def unit_row(half, unit):
    return unit if half == 0 else 5 - unit


def split(index, size):
    whole = jnp.floor((index + 0.5) * (1.0 / size))
    return whole, index - whole * size


def one_hot(picks, width):
    lane = lax.broadcasted_iota(jnp.int32, picks.shape, 1).astype(F32)
    tiles = [jnp.where(lane + at == picks, 1.0, 0.0) for at in range(0, width, 128)]
    return jnp.concatenate(tiles, axis=1)[:, 0:width].astype(BF16)


def index_of(rows):
    return lax.broadcasted_iota(jnp.int32, (rows, 128), 0).astype(F32)


def edge_picks():
    index = index_of(80)
    half, rest = split(index, 36)
    unit, rest = split(rest, 12)
    level, col = split(rest, 6)
    row = unit + half * (5 - 2 * unit)
    return jnp.where(index < 72, (level * 6 + row) * 48 + col, -1.0)


def window_picks():
    half, rest = split(index_of(576), 288)
    win, rest = split(rest, 72)
    unit, rest = split(rest, 24)
    level, col = split(rest, 12)
    row = unit + half * (5 - 2 * unit)
    at = win * 12 + 6 + col
    return jnp.where(at < 48, (level * 6 + row) * 48 + at, -1.0)


def window_edge_picks():
    group, col = split(index_of(144), 12)
    return jnp.where(col > 5.5, group * 6 + col - 6, -1.0)


def back_picks():
    group, col = split(index_of(48), 6)
    return group * 12 + 6 + col


def merge_picks():
    parity, rest = split(index_of(384), 96)
    col_parity, row_parity = split(parity, 2)
    s, rest = split(rest, 48)
    t, b = split(rest, 24)
    col = 2 * b + col_parity
    win, at = split(col - 6, 12)
    here = col > 5.5
    half = row_parity
    middle = jnp.where(here, s * 192 + (half * 4 + win) * 24 + t * 12 + at, -1.0)
    middle_edge = jnp.where(here, -1.0, ((s * 2 + half) * 2 + t) * 6 + col)
    unit = row_parity + t * (1 - 2 * row_parity)
    outer = jnp.where(here, (t * 4 + win) * 48 + unit * 24 + s * 12 + at, -1.0)
    outer_edge = jnp.where(here, -1.0, ((t * 2 + unit) * 2 + s) * 6 + col)
    return (middle, middle_edge), (outer, outer_edge)


def dot(a, b):
    return jnp.dot(a, b, preferred_element_type=F32)


def layer_norm(values):
    average = jnp.mean(values, axis=-1, keepdims=True)
    centred = values - average
    spread = jnp.mean(centred * centred, axis=-1, keepdims=True)
    return centred * lax.rsqrt(spread + 1e-05)


def attend(block, query_at, bias):
    head = lax.broadcasted_iota(jnp.int32, (48, 256), 1) // 64
    result = []
    for quad in range(2):
        at = 256 * quad
        query = block[pl.ds(query_at, 48), pl.ds(at, 256)] * 0.125
        query = jnp.concatenate([jnp.where(head == h, query, 0.0) for h in range(4)], axis=0)
        key = block[:, pl.ds(512 + at, 256)].astype(BF16)
        value = block[:, pl.ds(1024 + at, 256)].astype(BF16)
        scores = lax.dot_general(
            query.astype(BF16), key, (((1,), (1,)), ((), ())), preferred_element_type=F32
        )
        scores = scores + bias
        weights = jnp.exp(scores - jnp.max(scores, axis=-1, keepdims=True))
        total = jnp.sum(weights, axis=-1, keepdims=True)
        mixed = dot(weights.astype(BF16), value) / total
        picked = mixed[0:48]
        for h in range(1, 4):
            picked = jnp.where(head == h, mixed[48 * h : 48 * h + 48], picked)
        result.append(picked)
    return result


def band_biases(band_ids, lat, bias_own, bias_rim):
    seen, final = [], []
    for half in range(2):
        units = [unit_row(half, u) for u in range(3)] + ([-1, -2, -3] if half == 0 else [6, 7, 8])
        band = [band_ids[lax.rem(lat * 6 + u + 48, 48)] for u in units]

        def band_of(shape, dim):
            unit = lax.broadcasted_iota(jnp.int32, shape, dim) // 24
            held = jnp.full(shape, -1, jnp.int32)
            for u in range(5):
                held = jnp.where(unit == u, band[u], held)
            return held

        bias = jnp.where(band_of((96, 128), 0) == band_of((96, 128), 1), 0.0, NEVER)
        near = lax.broadcasted_iota(jnp.int32, (48, 128), 1) < 96
        for head in range(4):
            bias_own[half, pl.ds(48 * head, 48), :] = bias[0:48]
            bias_rim[half, pl.ds(48 * head, 48), :] = jnp.where(near, bias[48:96], NEVER)
        seen.append(jnp.full((1, WIDTH), band[2], jnp.int32) == band[3])
        final.append(jnp.full((1, WIDTH), band[0], jnp.int32) == band[5])
    return seen, final


def finish_chunk(restored, fc1, fc2, merge):
    base = restored.astype(F32)
    normed = layer_norm(base).astype(BF16)
    hidden = []
    for i in range(4):
        pre = dot(normed, fc1[:, pl.ds(512 * i, 512)])
        hidden.append((0.5 * pre * (1.0 + lax.erf(pre * 0.7071067811865476))).astype(BF16))
    done = (base + dot(jnp.concatenate(hidden, axis=1), fc2[...])).astype(BF16).astype(F32)
    pieces = [done[96 * i : 96 * i + 96] for i in range(4)]
    average = sum(jnp.sum(p, axis=-1, keepdims=True) for p in pieces) / 2048
    pieces = [p - average for p in pieces]
    spread = sum(jnp.sum(p * p, axis=-1, keepdims=True) for p in pieces) / 2048
    scale = lax.rsqrt(spread + 1e-05)
    return dot(jnp.concatenate([(p * scale).astype(BF16) for p in pieces], axis=1), merge[...])


def pack_chunk(merged, send):
    low = lax.broadcasted_iota(jnp.int32, (48, 128), 1) < 64
    for j in range(8):
        one = merged[0:48, 128 * j : 128 * j + 128]
        two = merged[48:96, 128 * j : 128 * j + 128]
        send[2 * j] = jnp.where(low, one, pltpu.roll(two, 64, 1)).astype(BF16)
        send[2 * j + 1] = jnp.where(low, pltpu.roll(one, 64, 1), two).astype(BF16)


def unpack_chunk(got, out, chunk):
    for t in range(2):
        lines = jnp.concatenate(
            [got[s].astype(F32)[24 * t : 24 * t + 24, :] for s in range(PEERS)], axis=0
        )
        turned = lines.T.astype(BF16)
        if chunk == 0:
            out[t, 1] = turned[0:64, :]
            out[2 + t, 1] = turned[64:128, :]
        else:
            out[2 * chunk - 2, 2 * t] = turned[0:64, :]
            out[2 * chunk - 1, 2 * t] = turned[64:128, :]


def kernel(
    tokens_hbm, qkv_hbm, proj_hbm, fc1_hbm, fc2_hbm, merge_hbm, band_ids,
    out,
    tokens, first, window, window_edge, back, middle, middle_edge, outer, outer_edge,
    qkv, proj, fc1, fc2, merge,
    edge_out, edge_in, placed, rim_out, rim_in, far_out, far_in, packed,
    middle_mixed, rim_mixed, outer_mixed, back_out, back_in, send, got, bias_own, bias_rim,
    token_sem, load_sem, edge_sem, rim_sem, far_sem, back_sem, send_sem, recv_sem, own_sem,
):
    sources = [qkv_hbm, proj_hbm, fc1_hbm, fc2_hbm, merge_hbm]
    places = [qkv, proj, fc1, fc2, merge]
    token_loads = [
        pltpu.make_async_copy(tokens_hbm.at[pl.ds(576 * g, 576)], tokens.at[g], token_sem.at[g])
        for g in range(2)
    ]
    loads = [
        pltpu.make_async_copy(src, dst, load_sem.at[i])
        for i, (src, dst) in enumerate(zip(sources, places))
    ]
    for load in token_loads + loads[:1]:
        load.start()

    lat = lax.axis_index("lat")
    lon = lax.axis_index("lon")
    up = {"lat": lax.rem(lat + LAT - 1, LAT)}
    down = {"lat": lax.rem(lat + 1, LAT)}
    west = {"lon": lax.rem(lon + PEERS - 1, PEERS)}
    east = {"lon": lax.rem(lon + 1, PEERS)}
    barrier = pltpu.get_barrier_semaphore()
    for to in (up, down):
        pl.semaphore_signal(barrier, inc=1, device_id=to, device_id_type=MESH)
    for d in range(1, PEERS):
        pl.semaphore_signal(
            barrier, inc=1, device_id={"lon": lax.rem(lon + d, PEERS)}, device_id_type=MESH
        )
    first[...] = one_hot(edge_picks(), 576)
    window[...] = one_hot(window_picks(), 576)
    window_edge[...] = one_hot(window_edge_picks(), 80)

    def remote(src, dst, sems, where, to):
        copy = pltpu.make_async_remote_copy(
            src_ref=src, dst_ref=dst, send_sem=sems.at[(0,) + where], recv_sem=sems.at[(1,) + where],
            device_id=to, device_id_type=MESH,
        )
        copy.start()
        return copy

    def send_rim(g, part):
        rows = (pl.ds(0, 64), pl.ds(64, 32))[part]
        return [
            remote(
                rim_out.at[g, half, rows], rim_in.at[g, 1 - half, rows],
                rim_sem, (g, half, part), (up, down)[half],
            )
            for half in range(2)
        ]

    def fill_rim(g, part):
        for half in range(2):
            at = 288 * half
            if part == 0:
                rows = [(at, 24), (at + 72, 24), (at + 144, 16)]
            else:
                rows = [(at + 160, 8), (at + 216, 24)]
            rim_out[g, half, pl.ds(64 * part, 64 - 32 * part), :] = jnp.concatenate(
                [placed[g, pl.ds(start, size), :] for start, size in rows], axis=0
            ).astype(BF16)

    def add_edge(g):
        edges[g].wait_recv()
        fresh = dot(window_edge[...], edge_in[g])
        for half in range(2):
            rows = pl.ds(288 * half + 216, 72)
            placed[g, rows, :] = placed[g, rows, :] + fresh[72 * half : 72 * half + 72]

    def own_qkv(blocks):
        values = jnp.concatenate([placed[g, pl.ds(72 * k, 72 * n), :] for g, k, n in blocks], axis=0)
        normed = layer_norm(values).astype(BF16)
        for part in range(3):
            cols = pl.ds(512 * part, 512)
            result = dot(normed, qkv[:, cols])
            at = 0
            for g, k, n in blocks:
                for i in range(n):
                    packed[g, k + i, pl.ds(0, 72), cols] = result[at : at + 72]
                    at += 72

    for g in range(2):
        token_loads[g].wait()
        edge_out[g] = dot(first[...], tokens[g]).astype(BF16)
    placed[0] = dot(window[...], tokens[0])
    fill_rim(0, 0)
    pl.semaphore_wait(barrier, PEERS + 1)
    edges = [remote(edge_out.at[g], edge_in.at[g], edge_sem, (g,), west) for g in range(2)]
    rims = [send_rim(0, 0), []]
    for load in loads[1:]:
        load.start()
    placed[1] = dot(window[...], tokens[1])
    fill_rim(1, 0)
    loads[0].wait()
    own_qkv([(0, 0, 3), (0, 4, 3)])
    add_edge(0)
    fill_rim(0, 1)
    rims[0] += send_rim(0, 1)
    rims[1] += send_rim(1, 0)
    add_edge(1)
    fill_rim(1, 1)
    rims[1] += send_rim(1, 1)
    own_qkv([(0, 3, 1), (0, 7, 1), (1, 3, 1), (1, 7, 1)])
    own_qkv([(1, 0, 3), (1, 4, 3)])
    for g in range(2):
        for k in range(8):
            packed[g, k, pl.ds(96, 32), :] = jnp.zeros((32, 1536), F32)
    edge_seen, edge_final = band_biases(band_ids, lat, bias_own, bias_rim)
    inner_picks, outer_picks = merge_picks()
    middle[...] = one_hot(inner_picks[0], 384)
    middle_edge[...] = one_hot(inner_picks[1], 48)
    outer[...] = one_hot(outer_picks[0], 384)
    outer_edge[...] = one_hot(outer_picks[1], 48)
    back[...] = one_hot(back_picks(), 96)
    fars = []
    for g in range(2):
        for copy in rims[g]:
            copy.wait_recv()
        rim = rim_in[g].reshape(192, WIDTH)
        normed = layer_norm(rim.astype(F32)).astype(BF16)
        for part in range(3):
            cols = pl.ds(512 * part, 512)
            result = dot(normed, qkv[:, cols])
            for k in range(8):
                packed[g, k, pl.ds(72, 24), cols] = result[24 * k : 24 * k + 24]
        for k in range(8):
            parts = attend(packed.at[g, k], 48, bias_rim[k // 4])
            for quad in range(2):
                cols = pl.ds(256 * quad, 256)
                middle_mixed[pl.ds(192 * g + 24 * k, 24), cols] = parts[quad][0:24]
                rim_mixed[g, pl.ds(24 * k, 24), cols] = parts[quad][24:48]
        for half in range(2):
            second = jnp.concatenate(
                [placed[g, pl.ds(288 * half + 72 * w + 24, 24), :] for w in range(4)], axis=0
            )
            far_out[g, half] = jnp.where(
                edge_seen[half], rim_mixed[g, pl.ds(96 * half, 96), :], second
            ).astype(BF16)
            fars.append(
                remote(far_out.at[g, half], far_in.at[g, 1 - half], far_sem, (g, half), (up, down)[half])
            )
    copies = []
    backs = []

    def project(mixed, own, chunk):
        fresh = own + dot(mixed.astype(BF16), proj[...])
        if chunk == 0:
            rim = [fresh[192 * g + 24 * k : 192 * g + 24 * k + 24] for g in range(2) for k in (3, 7)]
        else:
            rim = [fresh[48 * k : 48 * k + 48] for k in (3, 7)]
        back_out[chunk] = dot(back[...], jnp.concatenate(rim, axis=0).astype(BF16)).astype(BF16)
        backs.append(remote(back_out.at[chunk], back_in.at[chunk], back_sem, (chunk,), east))
        return fresh.astype(BF16)

    def finish(updated, chunk):
        order, order_edge = (middle, middle_edge) if chunk == 0 else (outer, outer_edge)
        inner = dot(order[...], updated)
        backs[chunk].wait_recv()
        restored = (inner + dot(order_edge[...], back_in[chunk])).astype(BF16)
        pack_chunk(finish_chunk(restored, fc1, fc2, merge), send.at[chunk])
        group = []
        for d in range(1, PEERS):
            to = lax.rem(lon + d, PEERS)
            copy = pltpu.make_async_remote_copy(
                src_ref=send.at[chunk, to], dst_ref=got.at[chunk, lon],
                send_sem=send_sem.at[chunk, d], recv_sem=recv_sem.at[chunk, d],
                device_id={"lon": to}, device_id_type=MESH,
            )
            copy.start()
            group.append(copy)
        copy = pltpu.make_async_copy(send.at[chunk, lon], got.at[chunk, lon], own_sem.at[chunk])
        copy.start()
        copies.append(group + [copy])

    def collect(chunk):
        for copy in copies[chunk]:
            copy.wait()
        unpack_chunk(got.at[chunk], out, chunk)

    loads[1].wait()
    own = jnp.concatenate(
        [placed[g, pl.ds(72 * k + 48, 24), :] for g in range(2) for k in range(8)], axis=0
    )
    updates = [project(middle_mixed[...], own, 0)]
    for load in loads[2:]:
        load.wait()
    for g in range(2):
        for half in range(2):
            fars[2 * g + half].wait_recv()
        far = far_in[g].reshape(192, WIDTH)
        normed = layer_norm(far.astype(F32)).astype(BF16)
        for part in range(1, 3):
            cols = pl.ds(512 * part, 512)
            result = dot(normed, qkv[:, cols])
            for k in range(8):
                packed[g, k, pl.ds(96, 24), cols] = result[24 * k : 24 * k + 24]
        for k in range(8):
            parts = attend(packed.at[g, k], 0, bias_own[k // 4])
            for quad in range(2):
                outer_mixed[pl.ds(48 * k, 48), pl.ds(256 * quad, 256)] = parts[quad]
        for half in range(2):
            final = far_in[g, half].astype(F32)
            for w in range(4):
                rows = pl.ds(192 * half + 48 * w, 24)
                outer_mixed[rows, :] = jnp.where(
                    edge_final[half], final[24 * w : 24 * w + 24], outer_mixed[rows, :]
                )
        own = jnp.concatenate([placed[g, pl.ds(72 * k, 48), :] for k in range(8)], axis=0)
        updates.append(project(outer_mixed[...], own, g + 1))
        if g == 0:
            finish(updates[0], 0)
    finish(updates[1], 1)
    collect(0)
    finish(updates[2], 2)
    collect(1)
    collect(2)
    for copy in edges + rims[0] + rims[1] + fars + backs:
        copy.wait_send()


def body(tokens, band_ids, qkv_weight, proj_weight, fc1_weight, fc2_weight, merge_weight):
    hbm = pl.BlockSpec(memory_space=pl.ANY)
    vmem = pl.BlockSpec(memory_space=pltpu.VMEM)
    dma = pltpu.SemaphoreType.DMA
    return pl.pallas_call(
        kernel,
        out_shape=jax.ShapeDtypeStruct((4, 3, 64, 384), BF16),
        in_specs=[hbm] * 6 + [pl.BlockSpec(memory_space=pltpu.SMEM)],
        out_specs=vmem,
        scratch_shapes=[
            pltpu.VMEM((2, 576, WIDTH), BF16),
            pltpu.VMEM((80, 576), BF16),
            pltpu.VMEM((576, 576), BF16),
            pltpu.VMEM((144, 80), BF16),
            pltpu.VMEM((48, 96), BF16),
            pltpu.VMEM((384, 384), BF16),
            pltpu.VMEM((384, 48), BF16),
            pltpu.VMEM((384, 384), BF16),
            pltpu.VMEM((384, 48), BF16),
            pltpu.VMEM((512, 1536), BF16),
            pltpu.VMEM((512, 512), BF16),
            pltpu.VMEM((512, 2048), BF16),
            pltpu.VMEM((2048, 512), BF16),
            pltpu.VMEM((2048, 1024), BF16),
            pltpu.VMEM((2, 80, WIDTH), BF16),
            pltpu.VMEM((2, 80, WIDTH), BF16),
            pltpu.VMEM((2, 576, WIDTH), F32),
            pltpu.VMEM((2, 2, 96, WIDTH), BF16),
            pltpu.VMEM((2, 2, 96, WIDTH), BF16),
            pltpu.VMEM((2, 2, 96, WIDTH), BF16),
            pltpu.VMEM((2, 2, 96, WIDTH), BF16),
            pltpu.VMEM((2, 8, 128, 1536), F32),
            pltpu.VMEM((384, WIDTH), F32),
            pltpu.VMEM((2, 192, WIDTH), F32),
            pltpu.VMEM((384, WIDTH), F32),
            pltpu.VMEM((3, 48, WIDTH), BF16),
            pltpu.VMEM((3, 48, WIDTH), BF16),
            pltpu.VMEM((3, PEERS, 48, 128), BF16),
            pltpu.VMEM((3, PEERS, 48, 128), BF16),
            pltpu.VMEM((2, 192, 128), F32),
            pltpu.VMEM((2, 192, 128), F32),
            dma((2,)),
            dma((5,)),
            dma((2, 2)),
            dma((2, 2, 2, 2)),
            dma((2, 2, 2)),
            dma((2, 3)),
            dma((3, PEERS)),
            dma((3, PEERS)),
            dma((3,)),
        ],
        compiler_params=pltpu.CompilerParams(
            collective_id=0, has_side_effects=True, vmem_limit_bytes=56 * 1024 * 1024
        ),
        name="layer",
    )(
        tokens.reshape(4 * 6 * 48, WIDTH),
        qkv_weight, proj_weight, fc1_weight, fc2_weight, merge_weight, band_ids,
    )


def solution(mesh):
    placed = (P(None, "lat", "lon", None), P(), P(), P(), P(), P(), P())
    return jax.shard_map(
        body, mesh=mesh, in_specs=placed, out_specs=P(None, "lat", "lon", None), check_vma=False
    )
```

```python
import jax
import jax.numpy as jnp
from jax import lax
from jax.experimental import pallas as pl
from jax.experimental.pallas import tpu as pltpu
from jax.sharding import PartitionSpec as P

MESH = pl.DeviceIdType.MESH
BF16 = jnp.bfloat16
F32 = jnp.float32
PEERS = 16
LAT = 8
WIDTH = 512
NEVER = -1e30


def unit_row(half, unit):
    return unit if half == 0 else 5 - unit


def split(index, size):
    whole = jnp.floor((index + 0.5) * (1.0 / size))
    return whole, index - whole * size


def one_hot(picks, width):
    lane = lax.broadcasted_iota(jnp.int32, picks.shape, 1).astype(F32)
    tiles = [jnp.where(lane + at == picks, 1.0, 0.0) for at in range(0, width, 128)]
    return jnp.concatenate(tiles, axis=1)[:, 0:width].astype(BF16)


def index_of(rows):
    return lax.broadcasted_iota(jnp.int32, (rows, 128), 0).astype(F32)


def edge_picks():
    index = index_of(80)
    half, rest = split(index, 36)
    unit, rest = split(rest, 12)
    level, col = split(rest, 6)
    row = unit + half * (5 - 2 * unit)
    return jnp.where(index < 72, (level * 6 + row) * 48 + col, -1.0)


def window_picks():
    half, rest = split(index_of(576), 288)
    win, rest = split(rest, 72)
    unit, rest = split(rest, 24)
    level, col = split(rest, 12)
    row = unit + half * (5 - 2 * unit)
    at = win * 12 + 6 + col
    return jnp.where(at < 48, (level * 6 + row) * 48 + at, -1.0)


def window_edge_picks():
    group, col = split(index_of(144), 12)
    return jnp.where(col > 5.5, group * 6 + col - 6, -1.0)


def back_picks():
    group, col = split(index_of(48), 6)
    return group * 12 + 6 + col


def merge_picks():
    parity, rest = split(index_of(384), 96)
    col_parity, row_parity = split(parity, 2)
    s, rest = split(rest, 48)
    t, b = split(rest, 24)
    col = 2 * b + col_parity
    win, at = split(col - 6, 12)
    here = col > 5.5
    half = row_parity
    middle = jnp.where(here, s * 192 + (half * 4 + win) * 24 + t * 12 + at, -1.0)
    middle_edge = jnp.where(here, -1.0, ((s * 2 + half) * 2 + t) * 6 + col)
    unit = row_parity + t * (1 - 2 * row_parity)
    outer = jnp.where(here, (t * 4 + win) * 48 + unit * 24 + s * 12 + at, -1.0)
    outer_edge = jnp.where(here, -1.0, ((t * 2 + unit) * 2 + s) * 6 + col)
    return (middle, middle_edge), (outer, outer_edge)


def dot(a, b):
    return jnp.dot(a, b, preferred_element_type=F32)


def layer_norm(values):
    average = jnp.mean(values, axis=-1, keepdims=True)
    centred = values - average
    spread = jnp.mean(centred * centred, axis=-1, keepdims=True)
    return centred * lax.rsqrt(spread + 1e-05)


def attend(block, query_at, bias):
    head = lax.broadcasted_iota(jnp.int32, (48, 256), 1) // 64
    result = []
    for quad in range(2):
        at = 256 * quad
        query = block[pl.ds(query_at, 48), pl.ds(at, 256)] * 0.125
        query = jnp.concatenate([jnp.where(head == h, query, 0.0) for h in range(4)], axis=0)
        key = block[:, pl.ds(512 + at, 256)].astype(BF16)
        value = block[:, pl.ds(1024 + at, 256)].astype(BF16)
        scores = lax.dot_general(
            query.astype(BF16), key, (((1,), (1,)), ((), ())), preferred_element_type=F32
        )
        scores = scores + bias
        weights = jnp.exp(scores - jnp.max(scores, axis=-1, keepdims=True))
        total = jnp.sum(weights, axis=-1, keepdims=True)
        mixed = dot(weights.astype(BF16), value) / total
        picked = mixed[0:48]
        for h in range(1, 4):
            picked = jnp.where(head == h, mixed[48 * h : 48 * h + 48], picked)
        result.append(picked)
    return result


def band_biases(band_ids, lat, bias_own, bias_rim):
    seen, final = [], []
    for half in range(2):
        units = [unit_row(half, u) for u in range(3)] + ([-1, -2, -3] if half == 0 else [6, 7, 8])
        band = [band_ids[lax.rem(lat * 6 + u + 48, 48)] for u in units]

        def band_of(shape, dim):
            unit = lax.broadcasted_iota(jnp.int32, shape, dim) // 24
            held = jnp.full(shape, -1, jnp.int32)
            for u in range(5):
                held = jnp.where(unit == u, band[u], held)
            return held

        bias = jnp.where(band_of((96, 128), 0) == band_of((96, 128), 1), 0.0, NEVER)
        near = lax.broadcasted_iota(jnp.int32, (48, 128), 1) < 96
        for head in range(4):
            bias_own[half, pl.ds(48 * head, 48), :] = bias[0:48]
            bias_rim[half, pl.ds(48 * head, 48), :] = jnp.where(near, bias[48:96], NEVER)
        seen.append(jnp.full((1, WIDTH), band[2], jnp.int32) == band[3])
        final.append(jnp.full((1, WIDTH), band[0], jnp.int32) == band[5])
    return seen, final


def finish_chunk(restored, fc1, fc2, merge):
    base = restored.astype(F32)
    normed = layer_norm(base).astype(BF16)
    hidden = []
    for i in range(4):
        pre = dot(normed, fc1[:, pl.ds(512 * i, 512)])
        hidden.append((0.5 * pre * (1.0 + lax.erf(pre * 0.7071067811865476))).astype(BF16))
    done = (base + dot(jnp.concatenate(hidden, axis=1), fc2[...])).astype(BF16).astype(F32)
    pieces = [done[96 * i : 96 * i + 96] for i in range(4)]
    average = sum(jnp.sum(p, axis=-1, keepdims=True) for p in pieces) / 2048
    pieces = [p - average for p in pieces]
    spread = sum(jnp.sum(p * p, axis=-1, keepdims=True) for p in pieces) / 2048
    scale = lax.rsqrt(spread + 1e-05)
    return dot(jnp.concatenate([(p * scale).astype(BF16) for p in pieces], axis=1), merge[...])


def pack_chunk(merged, send):
    low = lax.broadcasted_iota(jnp.int32, (48, 128), 1) < 64
    for j in range(8):
        one = merged[0:48, 128 * j : 128 * j + 128]
        two = merged[48:96, 128 * j : 128 * j + 128]
        send[2 * j] = jnp.where(low, one, pltpu.roll(two, 64, 1)).astype(BF16)
        send[2 * j + 1] = jnp.where(low, pltpu.roll(one, 64, 1), two).astype(BF16)


def unpack_chunk(got, out, chunk):
    for t in range(2):
        lines = jnp.concatenate(
            [got[s].astype(F32)[24 * t : 24 * t + 24, :] for s in range(PEERS)], axis=0
        )
        turned = lines.T.astype(BF16)
        if chunk == 0:
            out[t, 1] = turned[0:64, :]
            out[2 + t, 1] = turned[64:128, :]
        else:
            out[2 * chunk - 2, 2 * t] = turned[0:64, :]
            out[2 * chunk - 1, 2 * t] = turned[64:128, :]


def kernel(
    tokens_hbm, qkv_hbm, proj_hbm, fc1_hbm, fc2_hbm, merge_hbm, band_ids,
    got,
    tokens, first, window, window_edge, back, middle, middle_edge, outer, outer_edge,
    qkv, proj, fc1, fc2, merge,
    edge_out, edge_in, placed, rim_out, rim_in, far_out, far_in, packed,
    middle_mixed, rim_mixed, outer_mixed, back_out, back_in, send, bias_own, bias_rim,
    token_sem, load_sem, edge_sem, rim_sem, far_sem, back_sem, send_sem, recv_sem, own_sem,
):
    sources = [qkv_hbm, proj_hbm, fc1_hbm, fc2_hbm, merge_hbm]
    places = [qkv, proj, fc1, fc2, merge]
    token_loads = [
        pltpu.make_async_copy(tokens_hbm.at[pl.ds(576 * g, 576)], tokens.at[g], token_sem.at[g])
        for g in range(2)
    ]
    loads = [
        pltpu.make_async_copy(src, dst, load_sem.at[i])
        for i, (src, dst) in enumerate(zip(sources, places))
    ]
    for load in token_loads + loads[:1]:
        load.start()

    lat = lax.axis_index("lat")
    lon = lax.axis_index("lon")
    up = {"lat": lax.rem(lat + LAT - 1, LAT)}
    down = {"lat": lax.rem(lat + 1, LAT)}
    west = {"lon": lax.rem(lon + PEERS - 1, PEERS)}
    east = {"lon": lax.rem(lon + 1, PEERS)}
    barrier = pltpu.get_barrier_semaphore()
    for to in (up, down):
        pl.semaphore_signal(barrier, inc=1, device_id=to, device_id_type=MESH)
    for d in range(1, PEERS):
        pl.semaphore_signal(
            barrier, inc=1, device_id={"lon": lax.rem(lon + d, PEERS)}, device_id_type=MESH
        )
    first[...] = one_hot(edge_picks(), 576)
    window[...] = one_hot(window_picks(), 576)
    window_edge[...] = one_hot(window_edge_picks(), 80)

    def remote(src, dst, sems, where, to):
        copy = pltpu.make_async_remote_copy(
            src_ref=src, dst_ref=dst, send_sem=sems.at[(0,) + where], recv_sem=sems.at[(1,) + where],
            device_id=to, device_id_type=MESH,
        )
        copy.start()
        return copy

    def send_rim(g, part):
        rows = (pl.ds(0, 64), pl.ds(64, 32))[part]
        return [
            remote(
                rim_out.at[g, half, rows], rim_in.at[g, 1 - half, rows],
                rim_sem, (g, half, part), (up, down)[half],
            )
            for half in range(2)
        ]

    def fill_rim(g, part):
        for half in range(2):
            at = 288 * half
            if part == 0:
                rows = [(at, 24), (at + 72, 24), (at + 144, 16)]
            else:
                rows = [(at + 160, 8), (at + 216, 24)]
            rim_out[g, half, pl.ds(64 * part, 64 - 32 * part), :] = jnp.concatenate(
                [placed[g, pl.ds(start, size), :] for start, size in rows], axis=0
            ).astype(BF16)

    def add_edge(g):
        edges[g].wait_recv()
        fresh = dot(window_edge[...], edge_in[g])
        for half in range(2):
            rows = pl.ds(288 * half + 216, 72)
            placed[g, rows, :] = placed[g, rows, :] + fresh[72 * half : 72 * half + 72]

    def own_qkv(blocks):
        values = jnp.concatenate([placed[g, pl.ds(72 * k, 72 * n), :] for g, k, n in blocks], axis=0)
        normed = layer_norm(values).astype(BF16)
        for part in range(3):
            cols = pl.ds(512 * part, 512)
            result = dot(normed, qkv[:, cols])
            at = 0
            for g, k, n in blocks:
                for i in range(n):
                    packed[g, k + i, pl.ds(0, 72), cols] = result[at : at + 72]
                    at += 72

    for g in range(2):
        token_loads[g].wait()
        edge_out[g] = dot(first[...], tokens[g]).astype(BF16)
    placed[0] = dot(window[...], tokens[0])
    fill_rim(0, 0)
    pl.semaphore_wait(barrier, PEERS + 1)
    edges = [remote(edge_out.at[g], edge_in.at[g], edge_sem, (g,), west) for g in range(2)]
    rims = [send_rim(0, 0), []]
    for load in loads[1:]:
        load.start()
    placed[1] = dot(window[...], tokens[1])
    fill_rim(1, 0)
    loads[0].wait()
    own_qkv([(0, 0, 3), (0, 4, 3)])
    add_edge(0)
    fill_rim(0, 1)
    rims[0] += send_rim(0, 1)
    rims[1] += send_rim(1, 0)
    add_edge(1)
    fill_rim(1, 1)
    rims[1] += send_rim(1, 1)
    own_qkv([(0, 3, 1), (0, 7, 1), (1, 3, 1), (1, 7, 1)])
    own_qkv([(1, 0, 3), (1, 4, 3)])
    for g in range(2):
        for k in range(8):
            packed[g, k, pl.ds(96, 32), :] = jnp.zeros((32, 1536), F32)
    edge_seen, edge_final = band_biases(band_ids, lat, bias_own, bias_rim)
    inner_picks, outer_picks = merge_picks()
    middle[...] = one_hot(inner_picks[0], 384)
    middle_edge[...] = one_hot(inner_picks[1], 48)
    outer[...] = one_hot(outer_picks[0], 384)
    outer_edge[...] = one_hot(outer_picks[1], 48)
    back[...] = one_hot(back_picks(), 96)
    fars = []
    for g in range(2):
        for copy in rims[g]:
            copy.wait_recv()
        rim = rim_in[g].reshape(192, WIDTH)
        normed = layer_norm(rim.astype(F32)).astype(BF16)
        for part in range(3):
            cols = pl.ds(512 * part, 512)
            result = dot(normed, qkv[:, cols])
            for k in range(8):
                packed[g, k, pl.ds(72, 24), cols] = result[24 * k : 24 * k + 24]
        for k in range(8):
            parts = attend(packed.at[g, k], 48, bias_rim[k // 4])
            for quad in range(2):
                cols = pl.ds(256 * quad, 256)
                middle_mixed[pl.ds(192 * g + 24 * k, 24), cols] = parts[quad][0:24]
                rim_mixed[g, pl.ds(24 * k, 24), cols] = parts[quad][24:48]
        for half in range(2):
            second = jnp.concatenate(
                [placed[g, pl.ds(288 * half + 72 * w + 24, 24), :] for w in range(4)], axis=0
            )
            far_out[g, half] = jnp.where(
                edge_seen[half], rim_mixed[g, pl.ds(96 * half, 96), :], second
            ).astype(BF16)
            fars.append(
                remote(far_out.at[g, half], far_in.at[g, 1 - half], far_sem, (g, half), (up, down)[half])
            )
    copies = []
    backs = []

    def project(mixed, own, chunk):
        fresh = own + dot(mixed.astype(BF16), proj[...])
        if chunk == 0:
            rim = [fresh[192 * g + 24 * k : 192 * g + 24 * k + 24] for g in range(2) for k in (3, 7)]
        else:
            rim = [fresh[48 * k : 48 * k + 48] for k in (3, 7)]
        back_out[chunk] = dot(back[...], jnp.concatenate(rim, axis=0).astype(BF16)).astype(BF16)
        backs.append(remote(back_out.at[chunk], back_in.at[chunk], back_sem, (chunk,), east))
        return fresh.astype(BF16)

    def finish(updated, chunk):
        order, order_edge = (middle, middle_edge) if chunk == 0 else (outer, outer_edge)
        inner = dot(order[...], updated)
        backs[chunk].wait_recv()
        restored = (inner + dot(order_edge[...], back_in[chunk])).astype(BF16)
        pack_chunk(finish_chunk(restored, fc1, fc2, merge), send.at[chunk])
        group = []
        for d in range(1, PEERS):
            to = lax.rem(lon + d, PEERS)
            copy = pltpu.make_async_remote_copy(
                src_ref=send.at[chunk, to], dst_ref=got.at[chunk, lon],
                send_sem=send_sem.at[chunk, d], recv_sem=recv_sem.at[chunk, d],
                device_id={"lon": to}, device_id_type=MESH,
            )
            copy.start()
            group.append(copy)
        copy = pltpu.make_async_copy(send.at[chunk, lon], got.at[chunk, lon], own_sem.at[chunk])
        copy.start()
        copies.append(group + [copy])

    loads[1].wait()
    own = jnp.concatenate(
        [placed[g, pl.ds(72 * k + 48, 24), :] for g in range(2) for k in range(8)], axis=0
    )
    updates = [project(middle_mixed[...], own, 0)]
    for load in loads[2:]:
        load.wait()
    for g in range(2):
        for half in range(2):
            fars[2 * g + half].wait_recv()
        far = far_in[g].reshape(192, WIDTH)
        normed = layer_norm(far.astype(F32)).astype(BF16)
        for part in range(1, 3):
            cols = pl.ds(512 * part, 512)
            result = dot(normed, qkv[:, cols])
            for k in range(8):
                packed[g, k, pl.ds(96, 24), cols] = result[24 * k : 24 * k + 24]
        for k in range(8):
            parts = attend(packed.at[g, k], 0, bias_own[k // 4])
            for quad in range(2):
                outer_mixed[pl.ds(48 * k, 48), pl.ds(256 * quad, 256)] = parts[quad]
        for half in range(2):
            final = far_in[g, half].astype(F32)
            for w in range(4):
                rows = pl.ds(192 * half + 48 * w, 24)
                outer_mixed[rows, :] = jnp.where(
                    edge_final[half], final[24 * w : 24 * w + 24], outer_mixed[rows, :]
                )
        own = jnp.concatenate([placed[g, pl.ds(72 * k, 48), :] for k in range(8)], axis=0)
        updates.append(project(outer_mixed[...], own, g + 1))
        if g == 0:
            finish(updates[0], 0)
    finish(updates[1], 1)
    finish(updates[2], 2)
    for group in copies:
        for copy in group:
            copy.wait()
    for copy in edges + rims[0] + rims[1] + fars + backs:
        copy.wait_send()


def unpack_kernel(got, out):
    for chunk in range(3):
        unpack_chunk(got.at[chunk], out, chunk)


def body(tokens, band_ids, qkv_weight, proj_weight, fc1_weight, fc2_weight, merge_weight):
    hbm = pl.BlockSpec(memory_space=pl.ANY)
    vmem = pl.BlockSpec(memory_space=pltpu.VMEM)
    dma = pltpu.SemaphoreType.DMA
    got = pl.pallas_call(
        kernel,
        out_shape=jax.ShapeDtypeStruct((3, PEERS, 48, 128), BF16),
        in_specs=[hbm] * 6 + [pl.BlockSpec(memory_space=pltpu.SMEM)],
        out_specs=hbm,
        scratch_shapes=[
            pltpu.VMEM((2, 576, WIDTH), BF16),
            pltpu.VMEM((80, 576), BF16),
            pltpu.VMEM((576, 576), BF16),
            pltpu.VMEM((144, 80), BF16),
            pltpu.VMEM((48, 96), BF16),
            pltpu.VMEM((384, 384), BF16),
            pltpu.VMEM((384, 48), BF16),
            pltpu.VMEM((384, 384), BF16),
            pltpu.VMEM((384, 48), BF16),
            pltpu.VMEM((512, 1536), BF16),
            pltpu.VMEM((512, 512), BF16),
            pltpu.VMEM((512, 2048), BF16),
            pltpu.VMEM((2048, 512), BF16),
            pltpu.VMEM((2048, 1024), BF16),
            pltpu.VMEM((2, 80, WIDTH), BF16),
            pltpu.VMEM((2, 80, WIDTH), BF16),
            pltpu.VMEM((2, 576, WIDTH), F32),
            pltpu.VMEM((2, 2, 96, WIDTH), BF16),
            pltpu.VMEM((2, 2, 96, WIDTH), BF16),
            pltpu.VMEM((2, 2, 96, WIDTH), BF16),
            pltpu.VMEM((2, 2, 96, WIDTH), BF16),
            pltpu.VMEM((2, 8, 128, 1536), F32),
            pltpu.VMEM((384, WIDTH), F32),
            pltpu.VMEM((2, 192, WIDTH), F32),
            pltpu.VMEM((384, WIDTH), F32),
            pltpu.VMEM((3, 48, WIDTH), BF16),
            pltpu.VMEM((3, 48, WIDTH), BF16),
            pltpu.VMEM((3, PEERS, 48, 128), BF16),
            pltpu.VMEM((2, 192, 128), F32),
            pltpu.VMEM((2, 192, 128), F32),
            dma((2,)),
            dma((5,)),
            dma((2, 2)),
            dma((2, 2, 2, 2)),
            dma((2, 2, 2)),
            dma((2, 3)),
            dma((3, PEERS)),
            dma((3, PEERS)),
            dma((3,)),
        ],
        compiler_params=pltpu.CompilerParams(
            collective_id=0, has_side_effects=True, vmem_limit_bytes=56 * 1024 * 1024
        ),
        name="layer",
    )(
        tokens.reshape(4 * 6 * 48, WIDTH),
        qkv_weight, proj_weight, fc1_weight, fc2_weight, merge_weight, band_ids,
    )
    return pl.pallas_call(
        unpack_kernel,
        out_shape=jax.ShapeDtypeStruct((4, 3, 64, 384), BF16),
        in_specs=[vmem],
        out_specs=vmem,
        name="unpack",
    )(got)


def solution(mesh):
    placed = (P(None, "lat", "lon", None), P(), P(), P(), P(), P(), P())
    return jax.shard_map(
        body, mesh=mesh, in_specs=placed, out_specs=P(None, "lat", "lon", None), check_vma=False
    )
```

```python
import jax
import jax.numpy as jnp
from jax import lax
from jax.experimental import pallas as pl
from jax.experimental.pallas import tpu as pltpu
from jax.sharding import PartitionSpec as P

MESH = pl.DeviceIdType.MESH
BF16 = jnp.bfloat16
F32 = jnp.float32
PEERS = 16
LAT = 8
WIDTH = 512
NEVER = -1e30
FAR_FIRST = sorted(range(1, PEERS), key=lambda d: -min(d, PEERS - d))


def unit_row(half, unit):
    return unit if half == 0 else 5 - unit


def split(index, size):
    whole = jnp.floor((index + 0.5) * (1.0 / size))
    return whole, index - whole * size


def one_hot(picks, width):
    lane = lax.broadcasted_iota(jnp.int32, picks.shape, 1).astype(F32)
    tiles = [jnp.where(lane + at == picks, 1.0, 0.0) for at in range(0, width, 128)]
    return jnp.concatenate(tiles, axis=1)[:, 0:width].astype(BF16)


def index_of(rows):
    return lax.broadcasted_iota(jnp.int32, (rows, 128), 0).astype(F32)


def edge_picks():
    index = index_of(80)
    half, rest = split(index, 36)
    unit, rest = split(rest, 12)
    level, col = split(rest, 6)
    row = unit + half * (5 - 2 * unit)
    return jnp.where(index < 72, (level * 6 + row) * 48 + col, -1.0)


def window_picks():
    half, rest = split(index_of(576), 288)
    win, rest = split(rest, 72)
    unit, rest = split(rest, 24)
    level, col = split(rest, 12)
    row = unit + half * (5 - 2 * unit)
    at = win * 12 + 6 + col
    return jnp.where(at < 48, (level * 6 + row) * 48 + at, -1.0)


def window_edge_picks():
    group, col = split(index_of(144), 12)
    return jnp.where(col > 5.5, group * 6 + col - 6, -1.0)


def back_picks():
    group, col = split(index_of(48), 6)
    return group * 12 + 6 + col


def merge_picks():
    parity, rest = split(index_of(384), 96)
    col_parity, row_parity = split(parity, 2)
    s, rest = split(rest, 48)
    t, b = split(rest, 24)
    col = 2 * b + col_parity
    win, at = split(col - 6, 12)
    here = col > 5.5
    half = row_parity
    middle = jnp.where(here, s * 192 + (half * 4 + win) * 24 + t * 12 + at, -1.0)
    middle_edge = jnp.where(here, -1.0, ((s * 2 + half) * 2 + t) * 6 + col)
    unit = row_parity + t * (1 - 2 * row_parity)
    outer = jnp.where(here, (t * 4 + win) * 48 + unit * 24 + s * 12 + at, -1.0)
    outer_edge = jnp.where(here, -1.0, ((t * 2 + unit) * 2 + s) * 6 + col)
    return (middle, middle_edge), (outer, outer_edge)


def dot(a, b):
    return jnp.dot(a, b, preferred_element_type=F32)


def layer_norm(values):
    average = jnp.mean(values, axis=-1, keepdims=True)
    centred = values - average
    spread = jnp.mean(centred * centred, axis=-1, keepdims=True)
    return centred * lax.rsqrt(spread + 1e-05)


def attend(block, query_at, bias):
    head = lax.broadcasted_iota(jnp.int32, (48, 256), 1) // 64
    result = []
    for quad in range(2):
        at = 256 * quad
        query = block[pl.ds(query_at, 48), pl.ds(at, 256)] * 0.125
        query = jnp.concatenate([jnp.where(head == h, query, 0.0) for h in range(4)], axis=0)
        key = block[:, pl.ds(512 + at, 256)].astype(BF16)
        value = block[:, pl.ds(1024 + at, 256)].astype(BF16)
        scores = lax.dot_general(
            query.astype(BF16), key, (((1,), (1,)), ((), ())), preferred_element_type=F32
        )
        scores = scores + bias
        weights = jnp.exp(scores - jnp.max(scores, axis=-1, keepdims=True))
        total = jnp.sum(weights, axis=-1, keepdims=True)
        mixed = dot(weights.astype(BF16), value) / total
        picked = mixed[0:48]
        for h in range(1, 4):
            picked = jnp.where(head == h, mixed[48 * h : 48 * h + 48], picked)
        result.append(picked)
    return result


def band_biases(band_ids, lat, bias_own, bias_rim):
    seen, final = [], []
    for half in range(2):
        units = [unit_row(half, u) for u in range(3)] + ([-1, -2, -3] if half == 0 else [6, 7, 8])
        band = [band_ids[lax.rem(lat * 6 + u + 48, 48)] for u in units]

        def band_of(shape, dim):
            unit = lax.broadcasted_iota(jnp.int32, shape, dim) // 24
            held = jnp.full(shape, -1, jnp.int32)
            for u in range(5):
                held = jnp.where(unit == u, band[u], held)
            return held

        bias = jnp.where(band_of((96, 128), 0) == band_of((96, 128), 1), 0.0, NEVER)
        near = lax.broadcasted_iota(jnp.int32, (48, 128), 1) < 96
        for head in range(4):
            bias_own[half, pl.ds(48 * head, 48), :] = bias[0:48]
            bias_rim[half, pl.ds(48 * head, 48), :] = jnp.where(near, bias[48:96], NEVER)
        seen.append(jnp.full((1, WIDTH), band[2], jnp.int32) == band[3])
        final.append(jnp.full((1, WIDTH), band[0], jnp.int32) == band[5])
    return seen, final


def finish_chunk(restored, fc1, fc2, merge):
    base = restored.astype(F32)
    normed = layer_norm(base).astype(BF16)
    hidden = []
    for i in range(4):
        pre = dot(normed, fc1[:, pl.ds(512 * i, 512)])
        hidden.append((0.5 * pre * (1.0 + lax.erf(pre * 0.7071067811865476))).astype(BF16))
    done = (base + dot(jnp.concatenate(hidden, axis=1), fc2[...])).astype(BF16).astype(F32)
    pieces = [done[96 * i : 96 * i + 96] for i in range(4)]
    average = sum(jnp.sum(p, axis=-1, keepdims=True) for p in pieces) / 2048
    pieces = [p - average for p in pieces]
    spread = sum(jnp.sum(p * p, axis=-1, keepdims=True) for p in pieces) / 2048
    scale = lax.rsqrt(spread + 1e-05)
    return dot(jnp.concatenate([(p * scale).astype(BF16) for p in pieces], axis=1), merge[...])


def pack_chunk(merged, send):
    low = lax.broadcasted_iota(jnp.int32, (48, 128), 1) < 64
    for j in range(8):
        one = merged[0:48, 128 * j : 128 * j + 128]
        two = merged[48:96, 128 * j : 128 * j + 128]
        send[2 * j] = jnp.where(low, one, pltpu.roll(two, 64, 1)).astype(BF16)
        send[2 * j + 1] = jnp.where(low, pltpu.roll(one, 64, 1), two).astype(BF16)


def unpack_chunk(got, out, chunk):
    for t in range(2):
        lines = jnp.concatenate(
            [got[s].astype(F32)[24 * t : 24 * t + 24, :] for s in range(PEERS)], axis=0
        )
        turned = lines.T.astype(BF16)
        if chunk == 0:
            out[t, 1] = turned[0:64, :]
            out[2 + t, 1] = turned[64:128, :]
        else:
            out[2 * chunk - 2, 2 * t] = turned[0:64, :]
            out[2 * chunk - 1, 2 * t] = turned[64:128, :]


def kernel(
    tokens_hbm, qkv_hbm, proj_hbm, fc1_hbm, fc2_hbm, merge_hbm, band_ids,
    got,
    tokens, first, window, window_edge, back, middle, middle_edge, outer, outer_edge,
    qkv, proj, fc1, fc2, merge,
    edge_out, edge_in, placed, rim_out, rim_in, far_out, far_in, packed,
    middle_mixed, rim_mixed, outer_mixed, back_out, back_in, send, bias_own, bias_rim,
    token_sem, load_sem, edge_sem, rim_sem, far_sem, back_sem, send_sem, recv_sem,
):
    sources = [qkv_hbm, proj_hbm, fc1_hbm, fc2_hbm, merge_hbm]
    places = [qkv, proj, fc1, fc2, merge]
    token_loads = [
        pltpu.make_async_copy(tokens_hbm.at[pl.ds(576 * g, 576)], tokens.at[g], token_sem.at[g])
        for g in range(2)
    ]
    loads = [
        pltpu.make_async_copy(src, dst, load_sem.at[i])
        for i, (src, dst) in enumerate(zip(sources, places))
    ]
    for load in token_loads + loads[:1]:
        load.start()

    lat = lax.axis_index("lat")
    lon = lax.axis_index("lon")
    up = {"lat": lax.rem(lat + LAT - 1, LAT)}
    down = {"lat": lax.rem(lat + 1, LAT)}
    west = {"lon": lax.rem(lon + PEERS - 1, PEERS)}
    east = {"lon": lax.rem(lon + 1, PEERS)}
    barrier = pltpu.get_barrier_semaphore()
    for to in (up, down):
        pl.semaphore_signal(barrier, inc=1, device_id=to, device_id_type=MESH)
    for d in range(1, PEERS):
        pl.semaphore_signal(
            barrier, inc=1, device_id={"lon": lax.rem(lon + d, PEERS)}, device_id_type=MESH
        )
    first[...] = one_hot(edge_picks(), 576)
    window[...] = one_hot(window_picks(), 576)
    window_edge[...] = one_hot(window_edge_picks(), 80)

    def remote(src, dst, sems, where, to):
        copy = pltpu.make_async_remote_copy(
            src_ref=src, dst_ref=dst, send_sem=sems.at[(0,) + where], recv_sem=sems.at[(1,) + where],
            device_id=to, device_id_type=MESH,
        )
        copy.start()
        return copy

    def send_rim(g, part):
        rows = (pl.ds(0, 64), pl.ds(64, 32))[part]
        return [
            remote(
                rim_out.at[g, half, rows], rim_in.at[g, 1 - half, rows],
                rim_sem, (g, half, part), (up, down)[half],
            )
            for half in range(2)
        ]

    def fill_rim(g, part):
        for half in range(2):
            at = 288 * half
            if part == 0:
                rows = [(at, 24), (at + 72, 24), (at + 144, 16)]
            else:
                rows = [(at + 160, 8), (at + 216, 24)]
            rim_out[g, half, pl.ds(64 * part, 64 - 32 * part), :] = jnp.concatenate(
                [placed[g, pl.ds(start, size), :] for start, size in rows], axis=0
            ).astype(BF16)

    def add_edge(g):
        edges[g].wait_recv()
        fresh = dot(window_edge[...], edge_in[g])
        for half in range(2):
            rows = pl.ds(288 * half + 216, 72)
            placed[g, rows, :] = placed[g, rows, :] + fresh[72 * half : 72 * half + 72]

    def own_qkv(blocks):
        values = jnp.concatenate([placed[g, pl.ds(72 * k, 72 * n), :] for g, k, n in blocks], axis=0)
        normed = layer_norm(values).astype(BF16)
        for part in range(3):
            cols = pl.ds(512 * part, 512)
            result = dot(normed, qkv[:, cols])
            at = 0
            for g, k, n in blocks:
                for i in range(n):
                    packed[g, k + i, pl.ds(0, 72), cols] = result[at : at + 72]
                    at += 72

    for g in range(2):
        token_loads[g].wait()
        edge_out[g] = dot(first[...], tokens[g]).astype(BF16)
    placed[0] = dot(window[...], tokens[0])
    fill_rim(0, 0)
    pl.semaphore_wait(barrier, PEERS + 1)
    edges = [remote(edge_out.at[g], edge_in.at[g], edge_sem, (g,), west) for g in range(2)]
    rims = [send_rim(0, 0), []]
    for load in loads[1:]:
        load.start()
    placed[1] = dot(window[...], tokens[1])
    fill_rim(1, 0)
    loads[0].wait()
    own_qkv([(0, 0, 3), (0, 4, 3)])
    add_edge(0)
    fill_rim(0, 1)
    rims[0] += send_rim(0, 1)
    rims[1] += send_rim(1, 0)
    add_edge(1)
    fill_rim(1, 1)
    rims[1] += send_rim(1, 1)
    own_qkv([(0, 3, 1), (0, 7, 1), (1, 3, 1), (1, 7, 1)])
    own_qkv([(1, 0, 3), (1, 4, 3)])
    for g in range(2):
        for k in range(8):
            packed[g, k, pl.ds(96, 32), :] = jnp.zeros((32, 1536), F32)
    edge_seen, edge_final = band_biases(band_ids, lat, bias_own, bias_rim)
    inner_picks, outer_picks = merge_picks()
    middle[...] = one_hot(inner_picks[0], 384)
    middle_edge[...] = one_hot(inner_picks[1], 48)
    outer[...] = one_hot(outer_picks[0], 384)
    outer_edge[...] = one_hot(outer_picks[1], 48)
    back[...] = one_hot(back_picks(), 96)
    fars = []
    for g in range(2):
        for copy in rims[g]:
            copy.wait_recv()
        rim = rim_in[g].reshape(192, WIDTH)
        normed = layer_norm(rim.astype(F32)).astype(BF16)
        for part in range(3):
            cols = pl.ds(512 * part, 512)
            result = dot(normed, qkv[:, cols])
            for k in range(8):
                packed[g, k, pl.ds(72, 24), cols] = result[24 * k : 24 * k + 24]
        for k in range(8):
            parts = attend(packed.at[g, k], 48, bias_rim[k // 4])
            for quad in range(2):
                cols = pl.ds(256 * quad, 256)
                middle_mixed[pl.ds(192 * g + 24 * k, 24), cols] = parts[quad][0:24]
                rim_mixed[g, pl.ds(24 * k, 24), cols] = parts[quad][24:48]
        for half in range(2):
            second = jnp.concatenate(
                [placed[g, pl.ds(288 * half + 72 * w + 24, 24), :] for w in range(4)], axis=0
            )
            far_out[g, half] = jnp.where(
                edge_seen[half], rim_mixed[g, pl.ds(96 * half, 96), :], second
            ).astype(BF16)
            fars.append(
                remote(far_out.at[g, half], far_in.at[g, 1 - half], far_sem, (g, half), (up, down)[half])
            )
    backs = []

    def project(mixed, own, chunk):
        fresh = own + dot(mixed.astype(BF16), proj[...])
        if chunk == 0:
            rim = [fresh[192 * g + 24 * k : 192 * g + 24 * k + 24] for g in range(2) for k in (3, 7)]
        else:
            rim = [fresh[48 * k : 48 * k + 48] for k in (3, 7)]
        back_out[chunk] = dot(back[...], jnp.concatenate(rim, axis=0).astype(BF16)).astype(BF16)
        backs.append(remote(back_out.at[chunk], back_in.at[chunk], back_sem, (chunk,), east))
        return fresh.astype(BF16)

    def finish(updated, chunk):
        order, order_edge = (middle, middle_edge) if chunk == 0 else (outer, outer_edge)
        inner = dot(order[...], updated)
        backs[chunk].wait_recv()
        restored = (inner + dot(order_edge[...], back_in[chunk])).astype(BF16)
        pack_chunk(finish_chunk(restored, fc1, fc2, merge), send.at[chunk])
        for d in FAR_FIRST:
            to = lax.rem(lon + d, PEERS)
            copy = pltpu.make_async_remote_copy(
                src_ref=send.at[chunk, to], dst_ref=got.at[chunk, lon],
                send_sem=send_sem.at[chunk], recv_sem=recv_sem.at[chunk],
                device_id={"lon": to}, device_id_type=MESH,
            )
            copy.start()
        pltpu.make_async_copy(send.at[chunk, lon], got.at[chunk, lon], recv_sem.at[chunk]).start()

    loads[1].wait()
    own = jnp.concatenate(
        [placed[g, pl.ds(72 * k + 48, 24), :] for g in range(2) for k in range(8)], axis=0
    )
    updates = [project(middle_mixed[...], own, 0)]
    for load in loads[2:]:
        load.wait()
    for g in range(2):
        for half in range(2):
            fars[2 * g + half].wait_recv()
        far = far_in[g].reshape(192, WIDTH)
        normed = layer_norm(far.astype(F32)).astype(BF16)
        for part in range(1, 3):
            cols = pl.ds(512 * part, 512)
            result = dot(normed, qkv[:, cols])
            for k in range(8):
                packed[g, k, pl.ds(96, 24), cols] = result[24 * k : 24 * k + 24]
        for k in range(8):
            parts = attend(packed.at[g, k], 0, bias_own[k // 4])
            for quad in range(2):
                outer_mixed[pl.ds(48 * k, 48), pl.ds(256 * quad, 256)] = parts[quad]
        for half in range(2):
            final = far_in[g, half].astype(F32)
            for w in range(4):
                rows = pl.ds(192 * half + 48 * w, 24)
                outer_mixed[rows, :] = jnp.where(
                    edge_final[half], final[24 * w : 24 * w + 24], outer_mixed[rows, :]
                )
        own = jnp.concatenate([placed[g, pl.ds(72 * k, 48), :] for k in range(8)], axis=0)
        updates.append(project(outer_mixed[...], own, g + 1))
        if g == 0:
            finish(updates[0], 0)
    finish(updates[1], 1)
    finish(updates[2], 2)
    for chunk in range(3):
        sent = send.at[chunk, pl.ds(0, PEERS - 1)]
        pltpu.make_async_copy(sent, sent, send_sem.at[chunk]).wait()
        pltpu.make_async_copy(got.at[chunk], got.at[chunk], recv_sem.at[chunk]).wait()
    for copy in edges + rims[0] + rims[1] + fars + backs:
        copy.wait_send()


def unpack_kernel(got, out):
    for chunk in range(3):
        unpack_chunk(got.at[chunk], out, chunk)


def body(tokens, band_ids, qkv_weight, proj_weight, fc1_weight, fc2_weight, merge_weight):
    hbm = pl.BlockSpec(memory_space=pl.ANY)
    vmem = pl.BlockSpec(memory_space=pltpu.VMEM)
    dma = pltpu.SemaphoreType.DMA
    got = pl.pallas_call(
        kernel,
        out_shape=jax.ShapeDtypeStruct((3, PEERS, 48, 128), BF16),
        in_specs=[hbm] * 6 + [pl.BlockSpec(memory_space=pltpu.SMEM)],
        out_specs=hbm,
        scratch_shapes=[
            pltpu.VMEM((2, 576, WIDTH), BF16),
            pltpu.VMEM((80, 576), BF16),
            pltpu.VMEM((576, 576), BF16),
            pltpu.VMEM((144, 80), BF16),
            pltpu.VMEM((48, 96), BF16),
            pltpu.VMEM((384, 384), BF16),
            pltpu.VMEM((384, 48), BF16),
            pltpu.VMEM((384, 384), BF16),
            pltpu.VMEM((384, 48), BF16),
            pltpu.VMEM((512, 1536), BF16),
            pltpu.VMEM((512, 512), BF16),
            pltpu.VMEM((512, 2048), BF16),
            pltpu.VMEM((2048, 512), BF16),
            pltpu.VMEM((2048, 1024), BF16),
            pltpu.VMEM((2, 80, WIDTH), BF16),
            pltpu.VMEM((2, 80, WIDTH), BF16),
            pltpu.VMEM((2, 576, WIDTH), F32),
            pltpu.VMEM((2, 2, 96, WIDTH), BF16),
            pltpu.VMEM((2, 2, 96, WIDTH), BF16),
            pltpu.VMEM((2, 2, 96, WIDTH), BF16),
            pltpu.VMEM((2, 2, 96, WIDTH), BF16),
            pltpu.VMEM((2, 8, 128, 1536), F32),
            pltpu.VMEM((384, WIDTH), F32),
            pltpu.VMEM((2, 192, WIDTH), F32),
            pltpu.VMEM((384, WIDTH), F32),
            pltpu.VMEM((3, 48, WIDTH), BF16),
            pltpu.VMEM((3, 48, WIDTH), BF16),
            pltpu.VMEM((3, PEERS, 48, 128), BF16),
            pltpu.VMEM((2, 192, 128), F32),
            pltpu.VMEM((2, 192, 128), F32),
            dma((2,)),
            dma((5,)),
            dma((2, 2)),
            dma((2, 2, 2, 2)),
            dma((2, 2, 2)),
            dma((2, 3)),
            dma((3,)),
            dma((3,)),
        ],
        compiler_params=pltpu.CompilerParams(
            collective_id=0, has_side_effects=True, vmem_limit_bytes=56 * 1024 * 1024
        ),
        name="layer",
    )(
        tokens.reshape(4 * 6 * 48, WIDTH),
        qkv_weight, proj_weight, fc1_weight, fc2_weight, merge_weight, band_ids,
    )
    return pl.pallas_call(
        unpack_kernel,
        out_shape=jax.ShapeDtypeStruct((4, 3, 64, 384), BF16),
        in_specs=[vmem],
        out_specs=vmem,
        name="unpack",
    )(got)


def solution(mesh):
    placed = (P(None, "lat", "lon", None), P(), P(), P(), P(), P(), P())
    return jax.shard_map(
        body, mesh=mesh, in_specs=placed, out_specs=P(None, "lat", "lon", None), check_vma=False
    )
```

```python
import jax
import jax.numpy as jnp
from jax import lax
from jax.experimental import pallas as pl
from jax.experimental.pallas import tpu as pltpu
from jax.sharding import PartitionSpec as P

MESH = pl.DeviceIdType.MESH
BF16 = jnp.bfloat16
F32 = jnp.float32
PEERS = 16
LAT = 8
WIDTH = 512
NEVER = -1e30
FAR_FIRST = sorted(range(1, PEERS), key=lambda d: -min(d, PEERS - d))


def unit_row(half, unit):
    return unit if half == 0 else 5 - unit


def split(index, size):
    whole = jnp.floor((index + 0.5) * (1.0 / size))
    return whole, index - whole * size


def one_hot(picks, width):
    lane = lax.broadcasted_iota(jnp.int32, picks.shape, 1).astype(F32)
    tiles = [jnp.where(lane + at == picks, 1.0, 0.0) for at in range(0, width, 128)]
    return jnp.concatenate(tiles, axis=1)[:, 0:width].astype(BF16)


def index_of(rows):
    return lax.broadcasted_iota(jnp.int32, (rows, 128), 0).astype(F32)


def edge_picks():
    index = index_of(80)
    half, rest = split(index, 36)
    unit, rest = split(rest, 12)
    level, col = split(rest, 6)
    row = unit + half * (5 - 2 * unit)
    return jnp.where(index < 72, (level * 6 + row) * 48 + col, -1.0)


def window_picks():
    half, rest = split(index_of(576), 288)
    win, rest = split(rest, 72)
    unit, rest = split(rest, 24)
    level, col = split(rest, 12)
    row = unit + half * (5 - 2 * unit)
    at = win * 12 + 6 + col
    return jnp.where(at < 48, (level * 6 + row) * 48 + at, -1.0)


def window_edge_picks():
    group, col = split(index_of(144), 12)
    return jnp.where(col > 5.5, group * 6 + col - 6, -1.0)


def back_picks():
    group, col = split(index_of(48), 6)
    return group * 12 + 6 + col


def merge_picks():
    parity, rest = split(index_of(384), 96)
    col_parity, row_parity = split(parity, 2)
    s, rest = split(rest, 48)
    t, b = split(rest, 24)
    col = 2 * b + col_parity
    win, at = split(col - 6, 12)
    here = col > 5.5
    half = row_parity
    middle = jnp.where(here, s * 192 + (half * 4 + win) * 24 + t * 12 + at, -1.0)
    middle_edge = jnp.where(here, -1.0, ((s * 2 + half) * 2 + t) * 6 + col)
    unit = row_parity + t * (1 - 2 * row_parity)
    outer = jnp.where(here, (t * 4 + win) * 48 + unit * 24 + s * 12 + at, -1.0)
    outer_edge = jnp.where(here, -1.0, ((t * 2 + unit) * 2 + s) * 6 + col)
    return (middle, middle_edge), (outer, outer_edge)


def dot(a, b):
    return jnp.dot(a, b, preferred_element_type=F32)


def layer_norm(values):
    average = jnp.mean(values, axis=-1, keepdims=True)
    centred = values - average
    spread = jnp.mean(centred * centred, axis=-1, keepdims=True)
    return centred * lax.rsqrt(spread + 1e-05)


def attend(block, query_at, bias):
    head = lax.broadcasted_iota(jnp.int32, (48, 256), 1) // 64
    result = []
    for quad in range(2):
        at = 256 * quad
        query = block[pl.ds(query_at, 48), pl.ds(at, 256)] * 0.125
        query = jnp.concatenate([jnp.where(head == h, query, 0.0) for h in range(4)], axis=0)
        key = block[:, pl.ds(512 + at, 256)].astype(BF16)
        value = block[:, pl.ds(1024 + at, 256)].astype(BF16)
        scores = lax.dot_general(
            query.astype(BF16), key, (((1,), (1,)), ((), ())), preferred_element_type=F32
        )
        scores = scores + bias
        weights = jnp.exp(scores - jnp.max(scores, axis=-1, keepdims=True))
        total = jnp.sum(weights, axis=-1, keepdims=True)
        mixed = dot(weights.astype(BF16), value) / total
        picked = mixed[0:48]
        for h in range(1, 4):
            picked = jnp.where(head == h, mixed[48 * h : 48 * h + 48], picked)
        result.append(picked)
    return result


def band_biases(band_ids, lat, bias_own, bias_rim):
    seen, final = [], []
    for half in range(2):
        units = [unit_row(half, u) for u in range(3)] + ([-1, -2, -3] if half == 0 else [6, 7, 8])
        band = [band_ids[lax.rem(lat * 6 + u + 48, 48)] for u in units]

        def band_of(shape, dim):
            unit = lax.broadcasted_iota(jnp.int32, shape, dim) // 24
            held = jnp.full(shape, -1, jnp.int32)
            for u in range(5):
                held = jnp.where(unit == u, band[u], held)
            return held

        bias = jnp.where(band_of((96, 128), 0) == band_of((96, 128), 1), 0.0, NEVER)
        near = lax.broadcasted_iota(jnp.int32, (48, 128), 1) < 96
        for head in range(4):
            bias_own[half, pl.ds(48 * head, 48), :] = bias[0:48]
            bias_rim[half, pl.ds(48 * head, 48), :] = jnp.where(near, bias[48:96], NEVER)
        seen.append(jnp.full((1, WIDTH), band[2], jnp.int32) == band[3])
        final.append(jnp.full((1, WIDTH), band[0], jnp.int32) == band[5])
    return seen, final


def finish_chunk(restored, fc1, fc2, merge):
    base = restored.astype(F32)
    normed = layer_norm(base).astype(BF16)
    hidden = []
    for i in range(4):
        pre = dot(normed, fc1[:, pl.ds(512 * i, 512)])
        hidden.append((0.5 * pre * (1.0 + lax.erf(pre * 0.7071067811865476))).astype(BF16))
    done = (base + dot(jnp.concatenate(hidden, axis=1), fc2[...])).astype(BF16).astype(F32)
    pieces = [done[96 * i : 96 * i + 96] for i in range(4)]
    average = sum(jnp.sum(p, axis=-1, keepdims=True) for p in pieces) / 2048
    pieces = [p - average for p in pieces]
    spread = sum(jnp.sum(p * p, axis=-1, keepdims=True) for p in pieces) / 2048
    scale = lax.rsqrt(spread + 1e-05)
    return dot(jnp.concatenate([(p * scale).astype(BF16) for p in pieces], axis=1), merge[...])


def pack_chunk(merged, send):
    low = lax.broadcasted_iota(jnp.int32, (48, 128), 1) < 64
    for j in range(8):
        one = merged[0:48, 128 * j : 128 * j + 128]
        two = merged[48:96, 128 * j : 128 * j + 128]
        send[2 * j] = jnp.where(low, one, pltpu.roll(two, 64, 1)).astype(BF16)
        send[2 * j + 1] = jnp.where(low, pltpu.roll(one, 64, 1), two).astype(BF16)


def unpack_chunk(got, out, chunk):
    shape = (128, 128)
    same = jnp.where(
        lax.broadcasted_iota(jnp.int32, shape, 0) == lax.broadcasted_iota(jnp.int32, shape, 1), 1.0, 0.0
    ).astype(BF16)
    for t in range(2):
        lines = jnp.concatenate(
            [got[s].astype(F32)[24 * t : 24 * t + 24, :] for s in range(PEERS)], axis=0
        )
        turned = lax.dot_general(
            same, lines.astype(BF16), (((1,), (1,)), ((), ())), preferred_element_type=F32
        ).astype(BF16)
        if chunk == 0:
            out[t, 1] = turned[0:64, :]
            out[2 + t, 1] = turned[64:128, :]
        else:
            out[2 * chunk - 2, 2 * t] = turned[0:64, :]
            out[2 * chunk - 1, 2 * t] = turned[64:128, :]


def kernel(
    tokens_hbm, qkv_hbm, proj_hbm, fc1_hbm, fc2_hbm, merge_hbm, band_ids,
    got,
    tokens, first, window, window_edge, back, middle, middle_edge, outer, outer_edge,
    qkv, proj, fc1, fc2, merge,
    edge_out, edge_in, placed, rim_out, rim_in, far_out, far_in, packed,
    middle_mixed, rim_mixed, outer_mixed, back_out, back_in, send, bias_own, bias_rim,
    token_sem, load_sem, edge_sem, rim_sem, far_sem, back_sem, send_sem, recv_sem,
):
    sources = [qkv_hbm, proj_hbm, fc1_hbm, fc2_hbm, merge_hbm]
    places = [qkv, proj, fc1, fc2, merge]
    token_loads = [
        pltpu.make_async_copy(tokens_hbm.at[pl.ds(576 * g, 576)], tokens.at[g], token_sem.at[g])
        for g in range(2)
    ]
    loads = [
        pltpu.make_async_copy(src, dst, load_sem.at[i])
        for i, (src, dst) in enumerate(zip(sources, places))
    ]
    for load in token_loads + loads[:1]:
        load.start()

    lat = lax.axis_index("lat")
    lon = lax.axis_index("lon")
    up = {"lat": lax.rem(lat + LAT - 1, LAT)}
    down = {"lat": lax.rem(lat + 1, LAT)}
    west = {"lon": lax.rem(lon + PEERS - 1, PEERS)}
    east = {"lon": lax.rem(lon + 1, PEERS)}
    barrier = pltpu.get_barrier_semaphore()
    for to in (up, down):
        pl.semaphore_signal(barrier, inc=1, device_id=to, device_id_type=MESH)
    for d in range(1, PEERS):
        pl.semaphore_signal(
            barrier, inc=1, device_id={"lon": lax.rem(lon + d, PEERS)}, device_id_type=MESH
        )
    first[...] = one_hot(edge_picks(), 576)
    window[...] = one_hot(window_picks(), 576)
    window_edge[...] = one_hot(window_edge_picks(), 80)

    def remote(src, dst, sems, where, to):
        copy = pltpu.make_async_remote_copy(
            src_ref=src, dst_ref=dst, send_sem=sems.at[(0,) + where], recv_sem=sems.at[(1,) + where],
            device_id=to, device_id_type=MESH,
        )
        copy.start()
        return copy

    def send_rim(g, part):
        rows = (pl.ds(0, 64), pl.ds(64, 32))[part]
        return [
            remote(
                rim_out.at[g, half, rows], rim_in.at[g, 1 - half, rows],
                rim_sem, (g, half, part), (up, down)[half],
            )
            for half in range(2)
        ]

    def fill_rim(g, part):
        for half in range(2):
            at = 288 * half
            if part == 0:
                rows = [(at, 24), (at + 72, 24), (at + 144, 16)]
            else:
                rows = [(at + 160, 8), (at + 216, 24)]
            rim_out[g, half, pl.ds(64 * part, 64 - 32 * part), :] = jnp.concatenate(
                [placed[g, pl.ds(start, size), :] for start, size in rows], axis=0
            ).astype(BF16)

    def add_edge(g):
        edges[g].wait_recv()
        fresh = dot(window_edge[...], edge_in[g])
        for half in range(2):
            rows = pl.ds(288 * half + 216, 72)
            placed[g, rows, :] = placed[g, rows, :] + fresh[72 * half : 72 * half + 72]

    def own_qkv(blocks):
        values = jnp.concatenate([placed[g, pl.ds(72 * k, 72 * n), :] for g, k, n in blocks], axis=0)
        normed = layer_norm(values).astype(BF16)
        for part in range(3):
            cols = pl.ds(512 * part, 512)
            result = dot(normed, qkv[:, cols])
            at = 0
            for g, k, n in blocks:
                for i in range(n):
                    packed[g, k + i, pl.ds(0, 72), cols] = result[at : at + 72]
                    at += 72

    for g in range(2):
        token_loads[g].wait()
        edge_out[g] = dot(first[...], tokens[g]).astype(BF16)
    placed[0] = dot(window[...], tokens[0])
    fill_rim(0, 0)
    pl.semaphore_wait(barrier, PEERS + 1)
    edges = [remote(edge_out.at[g], edge_in.at[g], edge_sem, (g,), west) for g in range(2)]
    rims = [send_rim(0, 0), []]
    for load in loads[1:]:
        load.start()
    placed[1] = dot(window[...], tokens[1])
    fill_rim(1, 0)
    loads[0].wait()
    own_qkv([(0, 0, 3), (0, 4, 3)])
    add_edge(0)
    fill_rim(0, 1)
    rims[0] += send_rim(0, 1)
    rims[1] += send_rim(1, 0)
    add_edge(1)
    fill_rim(1, 1)
    rims[1] += send_rim(1, 1)
    own_qkv([(0, 3, 1), (0, 7, 1), (1, 3, 1), (1, 7, 1)])
    own_qkv([(1, 0, 3), (1, 4, 3)])
    for g in range(2):
        for k in range(8):
            packed[g, k, pl.ds(96, 32), :] = jnp.zeros((32, 1536), F32)
    edge_seen, edge_final = band_biases(band_ids, lat, bias_own, bias_rim)
    inner_picks, outer_picks = merge_picks()
    middle[...] = one_hot(inner_picks[0], 384)
    middle_edge[...] = one_hot(inner_picks[1], 48)
    outer[...] = one_hot(outer_picks[0], 384)
    outer_edge[...] = one_hot(outer_picks[1], 48)
    back[...] = one_hot(back_picks(), 96)
    fars = []
    for g in range(2):
        for copy in rims[g]:
            copy.wait_recv()
        rim = rim_in[g].reshape(192, WIDTH)
        normed = layer_norm(rim.astype(F32)).astype(BF16)
        for part in range(3):
            cols = pl.ds(512 * part, 512)
            result = dot(normed, qkv[:, cols])
            for k in range(8):
                packed[g, k, pl.ds(72, 24), cols] = result[24 * k : 24 * k + 24]
        for k in range(8):
            parts = attend(packed.at[g, k], 48, bias_rim[k // 4])
            for quad in range(2):
                cols = pl.ds(256 * quad, 256)
                middle_mixed[pl.ds(192 * g + 24 * k, 24), cols] = parts[quad][0:24]
                rim_mixed[g, pl.ds(24 * k, 24), cols] = parts[quad][24:48]
        for half in range(2):
            second = jnp.concatenate(
                [placed[g, pl.ds(288 * half + 72 * w + 24, 24), :] for w in range(4)], axis=0
            )
            far_out[g, half] = jnp.where(
                edge_seen[half], rim_mixed[g, pl.ds(96 * half, 96), :], second
            ).astype(BF16)
            fars.append(
                remote(far_out.at[g, half], far_in.at[g, 1 - half], far_sem, (g, half), (up, down)[half])
            )
    backs = []

    def project(mixed, own, chunk):
        fresh = own + dot(mixed.astype(BF16), proj[...])
        if chunk == 0:
            rim = [fresh[192 * g + 24 * k : 192 * g + 24 * k + 24] for g in range(2) for k in (3, 7)]
        else:
            rim = [fresh[48 * k : 48 * k + 48] for k in (3, 7)]
        back_out[chunk] = dot(back[...], jnp.concatenate(rim, axis=0).astype(BF16)).astype(BF16)
        backs.append(remote(back_out.at[chunk], back_in.at[chunk], back_sem, (chunk,), east))
        return fresh.astype(BF16)

    def finish(updated, chunk):
        order, order_edge = (middle, middle_edge) if chunk == 0 else (outer, outer_edge)
        inner = dot(order[...], updated)
        backs[chunk].wait_recv()
        restored = (inner + dot(order_edge[...], back_in[chunk])).astype(BF16)
        pack_chunk(finish_chunk(restored, fc1, fc2, merge), send.at[chunk])
        for d in FAR_FIRST:
            to = lax.rem(lon + d, PEERS)
            copy = pltpu.make_async_remote_copy(
                src_ref=send.at[chunk, to], dst_ref=got.at[chunk, lon],
                send_sem=send_sem.at[chunk], recv_sem=recv_sem.at[chunk],
                device_id={"lon": to}, device_id_type=MESH,
            )
            copy.start()
        pltpu.make_async_copy(send.at[chunk, lon], got.at[chunk, lon], recv_sem.at[chunk]).start()

    loads[1].wait()
    own = jnp.concatenate(
        [placed[g, pl.ds(72 * k + 48, 24), :] for g in range(2) for k in range(8)], axis=0
    )
    updates = [project(middle_mixed[...], own, 0)]
    for load in loads[2:]:
        load.wait()
    for g in range(2):
        for half in range(2):
            fars[2 * g + half].wait_recv()
        far = far_in[g].reshape(192, WIDTH)
        normed = layer_norm(far.astype(F32)).astype(BF16)
        for part in range(1, 3):
            cols = pl.ds(512 * part, 512)
            result = dot(normed, qkv[:, cols])
            for k in range(8):
                packed[g, k, pl.ds(96, 24), cols] = result[24 * k : 24 * k + 24]
        for k in range(8):
            parts = attend(packed.at[g, k], 0, bias_own[k // 4])
            for quad in range(2):
                outer_mixed[pl.ds(48 * k, 48), pl.ds(256 * quad, 256)] = parts[quad]
        for half in range(2):
            final = far_in[g, half].astype(F32)
            for w in range(4):
                rows = pl.ds(192 * half + 48 * w, 24)
                outer_mixed[rows, :] = jnp.where(
                    edge_final[half], final[24 * w : 24 * w + 24], outer_mixed[rows, :]
                )
        own = jnp.concatenate([placed[g, pl.ds(72 * k, 48), :] for k in range(8)], axis=0)
        updates.append(project(outer_mixed[...], own, g + 1))
        if g == 0:
            finish(updates[0], 0)
    finish(updates[1], 1)
    finish(updates[2], 2)
    for copy in edges + rims[0] + rims[1] + fars + backs:
        copy.wait_send()
    for chunk in range(3):
        sent = send.at[chunk, pl.ds(0, PEERS - 1)]
        pltpu.make_async_copy(sent, sent, send_sem.at[chunk]).wait()
        pltpu.make_async_copy(got.at[chunk], got.at[chunk], recv_sem.at[chunk]).wait()


def unpack_kernel(got, out):
    for chunk in range(3):
        unpack_chunk(got.at[chunk], out, chunk)


def body(tokens, band_ids, qkv_weight, proj_weight, fc1_weight, fc2_weight, merge_weight):
    hbm = pl.BlockSpec(memory_space=pl.ANY)
    vmem = pl.BlockSpec(memory_space=pltpu.VMEM)
    dma = pltpu.SemaphoreType.DMA
    got = pl.pallas_call(
        kernel,
        out_shape=jax.ShapeDtypeStruct((3, PEERS, 48, 128), BF16),
        in_specs=[hbm] * 6 + [pl.BlockSpec(memory_space=pltpu.SMEM)],
        out_specs=hbm,
        scratch_shapes=[
            pltpu.VMEM((2, 576, WIDTH), BF16),
            pltpu.VMEM((80, 576), BF16),
            pltpu.VMEM((576, 576), BF16),
            pltpu.VMEM((144, 80), BF16),
            pltpu.VMEM((48, 96), BF16),
            pltpu.VMEM((384, 384), BF16),
            pltpu.VMEM((384, 48), BF16),
            pltpu.VMEM((384, 384), BF16),
            pltpu.VMEM((384, 48), BF16),
            pltpu.VMEM((512, 1536), BF16),
            pltpu.VMEM((512, 512), BF16),
            pltpu.VMEM((512, 2048), BF16),
            pltpu.VMEM((2048, 512), BF16),
            pltpu.VMEM((2048, 1024), BF16),
            pltpu.VMEM((2, 80, WIDTH), BF16),
            pltpu.VMEM((2, 80, WIDTH), BF16),
            pltpu.VMEM((2, 576, WIDTH), F32),
            pltpu.VMEM((2, 2, 96, WIDTH), BF16),
            pltpu.VMEM((2, 2, 96, WIDTH), BF16),
            pltpu.VMEM((2, 2, 96, WIDTH), BF16),
            pltpu.VMEM((2, 2, 96, WIDTH), BF16),
            pltpu.VMEM((2, 8, 128, 1536), F32),
            pltpu.VMEM((384, WIDTH), F32),
            pltpu.VMEM((2, 192, WIDTH), F32),
            pltpu.VMEM((384, WIDTH), F32),
            pltpu.VMEM((3, 48, WIDTH), BF16),
            pltpu.VMEM((3, 48, WIDTH), BF16),
            pltpu.VMEM((3, PEERS, 48, 128), BF16),
            pltpu.VMEM((2, 192, 128), F32),
            pltpu.VMEM((2, 192, 128), F32),
            dma((2,)),
            dma((5,)),
            dma((2, 2)),
            dma((2, 2, 2, 2)),
            dma((2, 2, 2)),
            dma((2, 3)),
            dma((3,)),
            dma((3,)),
        ],
        compiler_params=pltpu.CompilerParams(
            collective_id=0, has_side_effects=True, vmem_limit_bytes=56 * 1024 * 1024
        ),
        name="layer",
    )(
        tokens.reshape(4 * 6 * 48, WIDTH),
        qkv_weight, proj_weight, fc1_weight, fc2_weight, merge_weight, band_ids,
    )
    return pl.pallas_call(
        unpack_kernel,
        out_shape=jax.ShapeDtypeStruct((4, 3, 64, 384), BF16),
        in_specs=[vmem],
        out_specs=vmem,
        name="unpack",
    )(got)


def solution(mesh):
    placed = (P(None, "lat", "lon", None), P(), P(), P(), P(), P(), P())
    return jax.shard_map(
        body, mesh=mesh, in_specs=placed, out_specs=P(None, "lat", "lon", None), check_vma=False
    )
```
